32 devices in a mesh: group: 2 (over y), dp: 8 (over z, x), latent: 2 (over core).
Axes of the slice: x: 2, y: 2, z: 4, core: 2. Of those that a mesh axis runs over, the one named last changes fastest.
Arguments:
- cur_rows: bfloat16 [32, 4608], P(('group', 'dp')), parts along dimension 0, may hold values from -144 to 144
- cached_rows: bfloat16 [32, 4608], P('group', 'dp'), parts along dimension 0, may hold values from -6 to 6
- shuffle_perm: int32 [32], P('group'), parts along dimension 0, may hold values from 0 to 15, each once
- weight: bfloat16 [8192, 4608], P(('group', 'dp', 'latent')), parts along dimension 0, may hold values from -0.09375 to 0.09375
- enc_bias: float32 [8192], P(('group', 'dp', 'latent')), parts along dimension 0, may hold values from -3 to 3
- dec_bias: float32 [9216], P('group'), parts along dimension 0, may hold values from -3 to 3
Outputs:
- weight_grad: bfloat16 [8192, 4608], P(('group', 'dp', 'latent')), parts along dimension 0
- enc_bias_grad: float32 [8192], P(('group', 'dp', 'latent')), parts along dimension 0
- dec_bias_grad: float32 [9216], P(('group', 'dp', 'latent')), parts along dimension 0
- next_batch: bfloat16 [32, 4608], P(('group', 'dp')), parts along dimension 0
The draws below stay inside these ranges and needn't reach their ends.
There are 2 independent parts, one for each index of `group`. The reference program is written for one: setup_inputs(seed, part) draws one part's arguments, and reference() takes and returns one part's arrays. A program takes and returns all parts, laid end to end along the dimension named above; each array names one. Nothing has to cross between parts.
Inputs may be any that keep to these rules, and one draw needn't show every extreme that they name: Cached row r goes to device shuffle_perm[r] // 2 of dp, slot shuffle_perm[r] % 2; every position once.
All inputs are finite; a program needn't handle non-finite values.
Results may differ from the reference program's by a relative error of at most 0.0055.
Values may be sent and summed in bfloat16 or wider, within the bound.
No kernel may reach another device: no remote copies, remote signals or barrier semaphores. Data moves between devices by JAX's collectives and lax.ppermute only.
A program may use at most 64 MiB of HBM per device.

```python
import math
import jax
import jax.numpy as jnp
from jax import lax

D = 4608
ROWS = 16
BATCH = 8
LATENTS = 4096


def draw_cur_rows(key, part):
    key = jax.random.fold_in(key, 11)
    key_base, key_rows, key_columns = jax.random.split(key, 3)
    position = jnp.arange(ROWS) % BATCH
    rising = 1.0 + 2.0 * position.astype(jnp.float32) / max(BATCH - 1, 1)
    spread = jnp.exp(jax.random.uniform(key_rows, (ROWS, 1), minval=0.0, maxval=math.log(4.0)))
    columns = jnp.exp(jax.random.uniform(key_columns, (1, D), minval=0.0, maxval=math.log(3.0)))
    values = jax.random.normal(key_base, (ROWS, D))
    values = jnp.clip(values, -4.0, 4.0)
    return (values * rising[:, None] * spread * columns).astype(jnp.bfloat16)


def block_levels(own_key, extent, cuts, least, top_value):
    loudness = 1.0
    for dim, shards_of in cuts:
        steps = jax.random.uniform(jax.random.fold_in(jax.random.fold_in(own_key, 6), dim), (shards_of,), jnp.float32, least / len(cuts), top_value / len(cuts))
        loudness = loudness * jnp.repeat(jnp.exp(steps), extent[dim] // shards_of).reshape((-1,) + (1,) * (len(extent) - 1 - dim))
    return loudness


def noise(stream_key, extent, scale, most, pieces=(), held_as=jnp.bfloat16):
    values = jax.random.normal(stream_key, extent, jnp.float32) * scale
    if len(pieces) > 0:
        values = block_levels(stream_key, extent, pieces, -0.22, 0.18) * values
    return jnp.clip(values, min=-most, max=most).astype(held_as)


def setup_inputs(seed: int = 0, part: int = 0) -> dict:
    arg_keys = jax.random.split(jax.random.key(seed), 7)
    part_keys = jax.random.split(jax.random.fold_in(arg_keys[6], part), 7)
    return {
        "cur_rows": draw_cur_rows(jax.random.fold_in(jax.random.fold_in(arg_keys[6], part), 71), part),
        "cached_rows": noise(part_keys[1], (ROWS, D), 1.0, 6.0, ((1, 8),)),
        "shuffle_perm": jax.random.permutation(part_keys[2], ROWS).astype(jnp.int32),
        "weight": noise(part_keys[3], (LATENTS, D), D ** -0.5, 0.09375, ((0, 16),)),
        "enc_bias": noise(part_keys[4], (LATENTS,), 0.5, 3.0, ((0, 16),), jnp.float32),
        "dec_bias": noise(part_keys[5], (D,), 0.5, 3.0, (), jnp.float32),
    }


SPARSITY = 4.0
SHARP = 4.0

def batch_scales(rows_f):
    squares = lax.optimization_barrier(jnp.sum(rows_f * rows_f, axis=1))
    batch_rows = squares.shape[0] // 2
    means = jnp.stack([jnp.mean(squares[:batch_rows]), jnp.mean(squares[batch_rows:])])
    scales = jnp.sqrt(rows_f.shape[1] / means)
    return jnp.repeat(scales, batch_rows)

def reference(cur_rows, cached_rows, shuffle_perm, weight, enc_bias, dec_bias):
    batch_rows = cur_rows.shape[0] // 2
    rows_f = cur_rows.astype(jnp.float32)
    scales = batch_scales(rows_f)
    projected = jnp.dot(cur_rows, weight.T, preferred_element_type=jnp.float32)
    preact = scales[:, None] * projected + enc_bias[None, :]
    latents = jax.nn.softplus(SHARP * preact) / SHARP
    latents_b = latents.astype(jnp.bfloat16)
    weight_f = weight.astype(jnp.float32)
    row_norms = jnp.sqrt(lax.optimization_barrier(jnp.sum(weight_f * weight_f, axis=1)) + 1e-06)
    recon = jnp.dot(latents_b, weight, preferred_element_type=jnp.float32) + dec_bias[None, :]
    error = recon - scales[:, None] * rows_f
    grad_out = (2.0 / batch_rows * error).astype(jnp.bfloat16)
    grad_latents = jnp.dot(grad_out, weight.T, preferred_element_type=jnp.float32) + SPARSITY / batch_rows * row_norms[None, :]
    grad_pre = grad_latents * jax.nn.sigmoid(SHARP * preact)
    enc_bias_grad = lax.optimization_barrier(jnp.sum(grad_pre, axis=0))
    scaled = (grad_pre * scales[:, None]).astype(jnp.bfloat16)
    left = jnp.concatenate([scaled, latents_b], axis=0)
    right = jnp.concatenate([cur_rows, grad_out], axis=0)
    summed = jnp.dot(left.T, right, preferred_element_type=jnp.float32)
    summed = summed + SPARSITY / batch_rows * lax.optimization_barrier(jnp.sum(latents, axis=0))[:, None] * weight_f / row_norms[:, None]
    weight_grad = summed.astype(jnp.bfloat16)
    dec_bias_grad = 2.0 / batch_rows * lax.optimization_barrier(jnp.sum(error, axis=0))
    next_batch = jnp.zeros_like(cached_rows).at[shuffle_perm].set(cached_rows)
    return (weight_grad, enc_bias_grad, dec_bias_grad, next_batch)
```

```python
import jax
import jax.numpy as jnp
from jax import lax
from jax.sharding import PartitionSpec as P

SPARSITY = 4.0
SHARP = 4.0


def batch_scales(rows_f):
    squares = jnp.sum(rows_f * rows_f, axis=1)
    batch_rows = squares.shape[0] // 2
    means = jnp.stack([jnp.mean(squares[:batch_rows]), jnp.mean(squares[batch_rows:])])
    scales = jnp.sqrt(rows_f.shape[1] / means)
    return jnp.repeat(scales, batch_rows)


def exchange(value, axis, distance):
    size = lax.axis_size(axis)
    return lax.ppermute(value, axis, [(k, k ^ distance) for k in range(size)])


def per_device(cur_rows, cached_rows, shuffle_perm, weight, enc_bias, dec_bias):
    dp = lax.axis_size("dp")
    own, width = cur_rows.shape
    half = width // 2
    core = lax.axis_index("latent")

    row_total, columns = cached_rows.shape
    slots = jnp.arange(row_total, dtype=jnp.int32)
    selector = (shuffle_perm[None, :] == slots[:, None]).astype(jnp.bfloat16)
    ordered = jnp.dot(selector, cached_rows, preferred_element_type=jnp.float32).astype(
        jnp.bfloat16
    )
    message = jnp.concatenate(
        [jnp.broadcast_to(cur_rows[None], (dp, own, width)), ordered.reshape(dp, own, columns)],
        axis=2,
    )
    arrived = lax.all_to_all(message, "dp", 0, 0)
    gathered = arrived[:, :, :width].reshape(dp * own, width)
    next_batch = arrived[:, :, width:].transpose(1, 0, 2).reshape(own, dp * columns)

    batch_rows = gathered.shape[0] // 2
    rows_f = gathered.astype(jnp.float32)
    scales = batch_scales(rows_f)
    projected = jnp.einsum("rd,ld->rl", gathered, weight, preferred_element_type=jnp.float32)
    preact = scales[:, None] * projected + enc_bias[None, :]
    latents = jax.nn.softplus(SHARP * preact) / SHARP
    latents_b = latents.astype(jnp.bfloat16)
    weight_f = weight.astype(jnp.float32)
    row_norms = jnp.sqrt(jnp.sum(weight_f * weight_f, axis=1) + 1e-06)

    partial = jnp.einsum("rl,ld->rd", latents_b, weight, preferred_element_type=jnp.float32)
    mine = lax.dynamic_slice_in_dim(partial, core * half, half, 1)
    other = lax.dynamic_slice_in_dim(partial, (1 - core) * half, half, 1)
    total = mine + exchange(other.astype(jnp.bfloat16), "latent", 1).astype(jnp.float32)
    distance = 1
    while distance < dp:
        total = total + exchange(total.astype(jnp.bfloat16), "dp", distance).astype(jnp.float32)
        distance *= 2

    target = lax.dynamic_slice_in_dim(rows_f, core * half, half, 1)
    bias = lax.dynamic_slice_in_dim(dec_bias, core * half, half, 0)
    error = total + bias[None, :] - target * scales[:, None]
    grad_mine = (2.0 / batch_rows * error).astype(jnp.bfloat16)
    grad_other = exchange(grad_mine, "latent", 1)
    low = jnp.where(core == 0, grad_mine, grad_other)
    high = jnp.where(core == 0, grad_other, grad_mine)
    grad_out = jnp.concatenate([low, high], axis=1)

    shares = width // (2 * dp)
    offset = lax.axis_index(("dp", "latent")) * shares
    column_sums = jnp.sum(grad_out.astype(jnp.float32), axis=0)
    dec_bias_grad = lax.dynamic_slice_in_dim(column_sums, offset, shares, 0)

    grad_latents = (
        jnp.einsum("rd,ld->rl", grad_out, weight, preferred_element_type=jnp.float32)
        + SPARSITY / batch_rows * row_norms[None, :]
    )
    grad_pre = grad_latents * jax.nn.sigmoid(SHARP * preact)
    enc_bias_grad = jnp.sum(grad_pre, axis=0)
    scaled = (grad_pre * scales[:, None]).astype(jnp.bfloat16)
    left = jnp.concatenate([scaled, latents_b], axis=0)
    right = jnp.concatenate([gathered, grad_out], axis=0)
    weight_sum = jnp.einsum("rl,rd->ld", left, right, preferred_element_type=jnp.float32)
    pull = SPARSITY / batch_rows * jnp.sum(latents, axis=0) / row_norms
    weight_grad = (weight_sum + pull[:, None] * weight_f).astype(jnp.bfloat16)
    return (weight_grad, enc_bias_grad, dec_bias_grad, next_batch)


def solution(mesh):
    return jax.shard_map(
        per_device,
        mesh=mesh,
        in_specs=(
            P(("group", "dp"), None),
            P("group", "dp"),
            P("group"),
            P(("group", "dp", "latent"), None),
            P(("group", "dp", "latent")),
            P("group"),
        ),
        out_specs=(
            P(("group", "dp", "latent"), None),
            P(("group", "dp", "latent")),
            P(("group", "dp", "latent")),
            P(("group", "dp"), None),
        ),
        check_vma=False,
    )
```

```python
import jax
import jax.numpy as jnp
from jax import lax
from jax.sharding import PartitionSpec as P

SPARSITY = 4.0
SHARP = 4.0


def batch_scales(rows_f):
    squares = jnp.sum(rows_f * rows_f, axis=1)
    batch_rows = squares.shape[0] // 2
    means = jnp.stack([jnp.mean(squares[:batch_rows]), jnp.mean(squares[batch_rows:])])
    scales = jnp.sqrt(rows_f.shape[1] / means)
    return jnp.repeat(scales, batch_rows)


def exchange(value, axis, distance):
    size = lax.axis_size(axis)
    return lax.ppermute(value, axis, [(k, k ^ distance) for k in range(size)])


def per_device(cur_rows, cached_rows, shuffle_perm, weight, enc_bias, dec_bias):
    dp = lax.axis_size("dp")
    own, width = cur_rows.shape
    half = width // 2
    core = lax.axis_index("latent")

    row_total, columns = cached_rows.shape
    slots = jnp.arange(row_total, dtype=jnp.int32)
    selector = (shuffle_perm[None, :] == slots[:, None]).astype(jnp.bfloat16)
    ordered = jnp.dot(selector, cached_rows, preferred_element_type=jnp.float32).astype(
        jnp.bfloat16
    )
    message = jnp.concatenate(
        [jnp.broadcast_to(cur_rows[None], (dp, own, width)), ordered.reshape(dp, own, columns)],
        axis=2,
    )
    arrived = lax.all_to_all(message, "dp", 0, 0)
    gathered = arrived[:, :, :width].reshape(dp * own, width)
    next_batch = arrived[:, :, width:].transpose(1, 0, 2).reshape(own, dp * columns)

    batch_rows = gathered.shape[0] // 2
    rows_f = gathered.astype(jnp.float32)
    scales = batch_scales(rows_f)
    projected = jnp.einsum("rd,ld->rl", gathered, weight, preferred_element_type=jnp.float32)
    preact = scales[:, None] * projected + enc_bias[None, :]
    latents = jax.nn.softplus(SHARP * preact) / SHARP
    latents_b = latents.astype(jnp.bfloat16)
    weight_f = weight.astype(jnp.float32)
    row_norms = jnp.sqrt(jnp.sum(weight_f * weight_f, axis=1) + 1e-06)

    partial = jnp.einsum("rl,ld->rd", latents_b, weight, preferred_element_type=jnp.float32)
    mine = lax.dynamic_slice_in_dim(partial, core * half, half, 1)
    other = lax.dynamic_slice_in_dim(partial, (1 - core) * half, half, 1)
    total = mine + exchange(other.astype(jnp.bfloat16), "latent", 1).astype(jnp.float32)
    corner = min(4, dp)
    sent = total.astype(jnp.bfloat16)
    for distance in range(1, corner):
        total = total + exchange(sent, "dp", distance).astype(jnp.float32)
    distance = corner
    while distance < dp:
        total = total + exchange(total.astype(jnp.bfloat16), "dp", distance).astype(jnp.float32)
        distance *= 2

    target = lax.dynamic_slice_in_dim(rows_f, core * half, half, 1)
    bias = lax.dynamic_slice_in_dim(dec_bias, core * half, half, 0)
    error = total + bias[None, :] - target * scales[:, None]
    grad_mine = (2.0 / batch_rows * error).astype(jnp.bfloat16)
    grad_other = exchange(grad_mine, "latent", 1)
    low = jnp.where(core == 0, grad_mine, grad_other)
    high = jnp.where(core == 0, grad_other, grad_mine)
    grad_out = jnp.concatenate([low, high], axis=1)

    shares = width // (2 * dp)
    offset = lax.axis_index(("dp", "latent")) * shares
    column_sums = jnp.sum(grad_out.astype(jnp.float32), axis=0)
    dec_bias_grad = lax.dynamic_slice_in_dim(column_sums, offset, shares, 0)

    grad_latents = (
        jnp.einsum("rd,ld->rl", grad_out, weight, preferred_element_type=jnp.float32)
        + SPARSITY / batch_rows * row_norms[None, :]
    )
    grad_pre = grad_latents * jax.nn.sigmoid(SHARP * preact)
    enc_bias_grad = jnp.sum(grad_pre, axis=0)
    scaled = (grad_pre * scales[:, None]).astype(jnp.bfloat16)
    left = jnp.concatenate([scaled, latents_b], axis=0)
    right = jnp.concatenate([gathered, grad_out], axis=0)
    weight_sum = jnp.einsum("rl,rd->ld", left, right, preferred_element_type=jnp.float32)
    pull = SPARSITY / batch_rows * jnp.sum(latents, axis=0) / row_norms
    weight_grad = (weight_sum + pull[:, None] * weight_f).astype(jnp.bfloat16)
    return (weight_grad, enc_bias_grad, dec_bias_grad, next_batch)


def solution(mesh):
    return jax.shard_map(
        per_device,
        mesh=mesh,
        in_specs=(
            P(("group", "dp"), None),
            P("group", "dp"),
            P("group"),
            P(("group", "dp", "latent"), None),
            P(("group", "dp", "latent")),
            P("group"),
        ),
        out_specs=(
            P(("group", "dp", "latent"), None),
            P(("group", "dp", "latent")),
            P(("group", "dp", "latent")),
            P(("group", "dp"), None),
        ),
        check_vma=False,
    )
```

```python
import functools

import jax
import jax.numpy as jnp
from jax import lax
from jax.experimental import pallas as pl
from jax.experimental.pallas import tpu as pltpu
from jax.sharding import PartitionSpec as P

SPARSITY = 4.0
SHARP = 4.0
VMEM_BYTES = 16 * 1024 * 1024
PACK_BYTES = 60 * 1024 * 1024
NT = (((1,), (1,)), ((), ()))
TN = (((0,), (0,)), ((), ()))


def whole(space=pltpu.VMEM):
    return pl.BlockSpec(memory_space=space)


def exchange(value, axis, distance):
    size = lax.axis_size(axis)
    return lax.ppermute(value, axis, [(k, k ^ distance) for k in range(size)])


def pack_kernel(cur_hbm, cached_hbm, perm_hbm, out_ref, cur_ref, cached_ref, perm_ref, sems):
    fetches = [
        pltpu.make_async_copy(source, target, sems.at[index])
        for index, (source, target) in enumerate(
            [(cur_hbm, cur_ref), (perm_hbm, perm_ref), (cached_hbm, cached_ref)]
        )
    ]
    for fetch in fetches:
        fetch.start()
    for fetch in fetches:
        fetch.wait()
    dp, own, _ = out_ref.shape
    width = cur_ref.shape[1]
    row_total = cached_ref.shape[0]
    slots = lax.broadcasted_iota(jnp.int32, (row_total, row_total), 0)
    selector = (jnp.broadcast_to(perm_ref[...], slots.shape) == slots).astype(jnp.bfloat16)
    ordered = jnp.dot(selector, cached_ref[...], preferred_element_type=jnp.float32)
    cur = cur_ref[...]
    for peer in range(dp):
        out_ref[peer, :, :width] = cur
        out_ref[peer, :, width:] = ordered[peer * own : (peer + 1) * own].astype(jnp.bfloat16)


def pack(cur_rows, cached_rows, shuffle_perm, dp):
    own, width = cur_rows.shape
    row_total, columns = cached_rows.shape
    return pl.pallas_call(
        pack_kernel,
        out_shape=jax.ShapeDtypeStruct((dp, own, width + columns), jnp.bfloat16),
        in_specs=[whole(pl.ANY)] * 3,
        out_specs=whole(),
        scratch_shapes=[
            pltpu.VMEM((own, width), jnp.bfloat16),
            pltpu.VMEM((row_total, columns), jnp.bfloat16),
            pltpu.VMEM((1, row_total), jnp.int32),
            pltpu.SemaphoreType.DMA((3,)),
        ],
        compiler_params=pltpu.CompilerParams(vmem_limit_bytes=PACK_BYTES),
        name="pack",
    )(cur_rows, cached_rows, shuffle_perm.reshape(1, row_total))


def encode_kernel(
    rows_ref,
    weight_ref,
    bias_ref,
    norms_ref,
    send_ref,
    mine_ref,
    latents_ref,
    gate_ref,
    scales_ref,
    pull_ref,
):
    rows_total, width = rows_ref.shape
    half = width // 2
    batch_rows = rows_total // 2
    core = lax.axis_index("latent")
    projected = lax.dot_general(
        rows_ref[...], weight_ref[...], NT, preferred_element_type=jnp.float32
    )
    rows_f = rows_ref[...].astype(jnp.float32)
    squares = jnp.sum(rows_f * rows_f, axis=1, keepdims=True)
    first = jnp.sum(squares[:batch_rows], axis=0, keepdims=True) / batch_rows
    second = jnp.sum(squares[batch_rows:], axis=0, keepdims=True) / batch_rows
    row = lax.broadcasted_iota(jnp.int32, (rows_total, 1), 0)
    scales = jnp.sqrt(width / jnp.where(row < batch_rows, first, second))
    scales_ref[...] = scales
    sharp = SHARP * (scales * projected + bias_ref[...])
    latents = jax.nn.softplus(sharp) / SHARP
    latents_ref[...] = latents
    gate_ref[...] = jax.nn.sigmoid(sharp)
    counts = jnp.sum(latents, axis=0, keepdims=True)
    pull_ref[...] = SPARSITY / batch_rows * counts / norms_ref[...]
    latents_b = latents.astype(jnp.bfloat16)
    there = pl.multiple_of((1 - core) * half, 128)
    here = pl.multiple_of(core * half, 128)
    send_ref[...] = jnp.dot(
        latents_b, weight_ref[:, pl.ds(there, half)], preferred_element_type=jnp.float32
    ).astype(jnp.bfloat16)
    mine_ref[...] = jnp.dot(
        latents_b, weight_ref[:, pl.ds(here, half)], preferred_element_type=jnp.float32
    )


def encode(rows, weight, enc_bias, norms):
    rows_total, width = rows.shape
    count = weight.shape[0]
    f32 = jnp.float32
    return pl.pallas_call(
        encode_kernel,
        out_shape=(
            jax.ShapeDtypeStruct((rows_total, width // 2), jnp.bfloat16),
            jax.ShapeDtypeStruct((rows_total, width // 2), f32),
            jax.ShapeDtypeStruct((rows_total, count), f32),
            jax.ShapeDtypeStruct((rows_total, count), f32),
            jax.ShapeDtypeStruct((rows_total, 1), f32),
            jax.ShapeDtypeStruct((1, count), f32),
        ),
        in_specs=[whole()] * 4,
        out_specs=[whole()] * 6,
        compiler_params=pltpu.CompilerParams(vmem_limit_bytes=VMEM_BYTES),
        name="encode",
    )(rows, weight, enc_bias.reshape(1, count), norms)


def finish_kernel(
    tile,
    low_ref,
    high_ref,
    rows_ref,
    weight_ref,
    latents_ref,
    gate_ref,
    scales_ref,
    norms_ref,
    pull_ref,
    weight_grad_ref,
    bias_grad_ref,
    staged_ref,
    sems,
):
    rows_total, width = rows_ref.shape
    half = width // 2
    batch_rows = rows_total // 2
    grad_latents = (
        lax.dot_general(
            low_ref[...], weight_ref[:, :half], NT, preferred_element_type=jnp.float32
        )
        + lax.dot_general(
            high_ref[...], weight_ref[:, half:], NT, preferred_element_type=jnp.float32
        )
        + SPARSITY / batch_rows * norms_ref[...]
    )
    grad_pre = grad_latents * gate_ref[...]
    bias_grad_ref[...] = jnp.sum(grad_pre, axis=0, keepdims=True)
    scaled = (grad_pre * scales_ref[...]).astype(jnp.bfloat16)
    left = jnp.concatenate([scaled, latents_ref[...].astype(jnp.bfloat16)], axis=0)
    pull = pull_ref[...]
    copies = []
    for index in range(width // tile):
        start = index * tile
        columns = slice(start, start + tile)
        if start < half:
            grad = low_ref[:, columns]
        else:
            grad = high_ref[:, start - half : start - half + tile]
        right = jnp.concatenate([rows_ref[:, columns], grad], axis=0)
        total = lax.dot_general(left, right, TN, preferred_element_type=jnp.float32)
        total = total + pull * weight_ref[:, columns].astype(jnp.float32)
        staged_ref[:, columns] = total.astype(jnp.bfloat16)
        copy = pltpu.make_async_copy(
            staged_ref.at[:, columns], weight_grad_ref.at[:, columns], sems.at[index]
        )
        copy.start()
        copies.append(copy)
    for copy in copies:
        copy.wait()


def finish(low, high, rows, weight, latents, gate, scales, norms, pull):
    rows_total, width = rows.shape
    count = weight.shape[0]
    tile = 384
    return pl.pallas_call(
        functools.partial(finish_kernel, tile),
        out_shape=(
            jax.ShapeDtypeStruct((count, width), jnp.bfloat16),
            jax.ShapeDtypeStruct((1, count), jnp.float32),
        ),
        in_specs=[whole()] * 9,
        out_specs=[whole(pl.ANY), whole()],
        scratch_shapes=[
            pltpu.VMEM((count, width), jnp.bfloat16),
            pltpu.SemaphoreType.DMA((width // tile,)),
        ],
        compiler_params=pltpu.CompilerParams(vmem_limit_bytes=VMEM_BYTES),
        name="finish",
    )(low, high, rows, weight, latents, gate, scales, norms, pull)


def per_device(cur_rows, cached_rows, shuffle_perm, weight, enc_bias, dec_bias):
    dp = lax.axis_size("dp")
    own, width = cur_rows.shape
    columns = cached_rows.shape[1]
    half = width // 2
    count = weight.shape[0]
    batch_rows = dp * own // 2
    core = lax.axis_index("latent")

    arrived = lax.all_to_all(pack(cur_rows, cached_rows, shuffle_perm, dp), "dp", 0, 0)
    gathered = arrived[:, :, :width].reshape(dp * own, width)
    next_batch = arrived[:, :, width:].transpose(1, 0, 2).reshape(own, dp * columns)

    weight_f = weight.astype(jnp.float32)
    norms = jnp.sqrt(jnp.sum(weight_f * weight_f, axis=1) + 1e-06).reshape(1, count)
    send, mine, latents, gate, scales, pull = encode(gathered, weight, enc_bias, norms)

    total = mine + exchange(send, "latent", 1).astype(jnp.float32)
    corner = min(4, dp)
    sent = total.astype(jnp.bfloat16)
    for distance in range(1, corner):
        total = total + exchange(sent, "dp", distance).astype(jnp.float32)
    distance = corner
    while distance < dp:
        total = total + exchange(total.astype(jnp.bfloat16), "dp", distance).astype(jnp.float32)
        distance *= 2

    target = lax.dynamic_slice_in_dim(gathered, core * half, half, 1).astype(jnp.float32)
    bias = lax.dynamic_slice_in_dim(dec_bias, core * half, half, 0)
    error = total + bias[None, :] - target * scales
    grad_mine = (2.0 / batch_rows * error).astype(jnp.bfloat16)
    grad_other = exchange(grad_mine, "latent", 1)
    low = jnp.where(core == 0, grad_mine, grad_other)
    high = jnp.where(core == 0, grad_other, grad_mine)

    shares = width // (2 * dp)
    offset = lax.axis_index(("dp", "latent")) * shares
    column_sums = jnp.concatenate(
        [jnp.sum(low.astype(jnp.float32), axis=0), jnp.sum(high.astype(jnp.float32), axis=0)]
    )
    dec_bias_grad = lax.dynamic_slice_in_dim(column_sums, offset, shares, 0)

    weight_grad, enc_bias_grad = finish(
        low,
        high,
        gathered,
        weight,
        latents,
        gate,
        scales,
        norms,
        pull.reshape(count, 1),
    )
    return (weight_grad, enc_bias_grad.reshape(count), dec_bias_grad, next_batch)


def solution(mesh):
    return jax.shard_map(
        per_device,
        mesh=mesh,
        in_specs=(
            P(("group", "dp"), None),
            P("group", "dp"),
            P("group"),
            P(("group", "dp", "latent"), None),
            P(("group", "dp", "latent")),
            P("group"),
        ),
        out_specs=(
            P(("group", "dp", "latent"), None),
            P(("group", "dp", "latent")),
            P(("group", "dp", "latent")),
            P(("group", "dp"), None),
        ),
        check_vma=False,
    )
```

```python
import functools

import jax
import jax.numpy as jnp
from jax import lax
from jax.experimental import pallas as pl
from jax.experimental.pallas import tpu as pltpu
from jax.sharding import PartitionSpec as P

SPARSITY = 4.0
SHARP = 4.0
VMEM_BYTES = 16 * 1024 * 1024
PACK_BYTES = 60 * 1024 * 1024
NT = (((1,), (1,)), ((), ()))
TN = (((0,), (0,)), ((), ()))


def whole(space=pltpu.VMEM):
    return pl.BlockSpec(memory_space=space)


def exchange(value, axis, distance):
    size = lax.axis_size(axis)
    return lax.ppermute(value, axis, [(k, k ^ distance) for k in range(size)])


def core_columns(half):
    core = lax.axis_index("latent")
    here = pl.ds(pl.multiple_of(core * half, 128), half)
    there = pl.ds(pl.multiple_of((1 - core) * half, 128), half)
    return here, there


def pack_kernel(cur_hbm, cached_hbm, perm_hbm, out_hbm, cached_ref, perm_ref, ordered_ref, sems):
    dp, own, _ = out_hbm.shape
    width = cur_hbm.shape[1]
    row_total, columns = cached_ref.shape
    fetches = [
        pltpu.make_async_copy(cached_hbm, cached_ref, sems.at[0]),
        pltpu.make_async_copy(perm_hbm, perm_ref, sems.at[1]),
    ]
    for fetch in fetches:
        fetch.start()
    spreads = [
        pltpu.make_async_copy(cur_hbm, out_hbm.at[peer, :, pl.ds(0, width)], sems.at[3 + peer])
        for peer in range(dp)
    ]
    for spread in spreads:
        spread.start()
    for fetch in fetches:
        fetch.wait()
    slots = lax.broadcasted_iota(jnp.int32, (row_total, row_total), 0)
    selector = (jnp.broadcast_to(perm_ref[...], slots.shape) == slots).astype(jnp.bfloat16)
    ordered = jnp.dot(selector, cached_ref[...], preferred_element_type=jnp.float32)
    for peer in range(dp):
        ordered_ref[peer] = ordered[peer * own : (peer + 1) * own].astype(jnp.bfloat16)
    last = pltpu.make_async_copy(
        ordered_ref, out_hbm.at[:, :, pl.ds(width, columns)], sems.at[2]
    )
    last.start()
    for spread in spreads:
        spread.wait()
    last.wait()


def pack(cur_rows, cached_rows, shuffle_perm, dp):
    own, width = cur_rows.shape
    row_total, columns = cached_rows.shape
    return pl.pallas_call(
        pack_kernel,
        out_shape=jax.ShapeDtypeStruct((dp, own, width + columns), jnp.bfloat16),
        in_specs=[whole(pl.ANY)] * 3,
        out_specs=whole(pl.ANY),
        scratch_shapes=[
            pltpu.VMEM((row_total, columns), jnp.bfloat16),
            pltpu.VMEM((1, row_total), jnp.int32),
            pltpu.VMEM((dp, own, columns), jnp.bfloat16),
            pltpu.SemaphoreType.DMA((3 + dp,)),
        ],
        compiler_params=pltpu.CompilerParams(vmem_limit_bytes=PACK_BYTES),
        name="pack",
    )(cur_rows, cached_rows, shuffle_perm.reshape(1, row_total))


def encode_kernel(rows_ref, weight_ref, bias_ref, send_ref, latents_ref, sharp_ref, scales_ref):
    rows_total, width = rows_ref.shape
    batch_rows = rows_total // 2
    projected = lax.dot_general(
        rows_ref[...], weight_ref[...], NT, preferred_element_type=jnp.float32
    )
    rows_f = rows_ref[...].astype(jnp.float32)
    squares = jnp.sum(rows_f * rows_f, axis=1, keepdims=True)
    first = jnp.sum(squares[:batch_rows], axis=0, keepdims=True) / batch_rows
    second = jnp.sum(squares[batch_rows:], axis=0, keepdims=True) / batch_rows
    row = lax.broadcasted_iota(jnp.int32, (rows_total, 1), 0)
    scales = jnp.sqrt(width / jnp.where(row < batch_rows, first, second))
    scales_ref[...] = scales
    sharp = SHARP * (scales * projected + bias_ref[...])
    latents = jax.nn.softplus(sharp) / SHARP
    sharp_ref[...] = sharp
    latents_ref[...] = latents
    _, there = core_columns(width // 2)
    send_ref[...] = jnp.dot(
        latents.astype(jnp.bfloat16), weight_ref[:, there], preferred_element_type=jnp.float32
    ).astype(jnp.bfloat16)


def encode(rows, weight, enc_bias):
    rows_total, width = rows.shape
    count = weight.shape[0]
    f32 = jnp.float32
    return pl.pallas_call(
        encode_kernel,
        out_shape=(
            jax.ShapeDtypeStruct((rows_total, width // 2), jnp.bfloat16),
            jax.ShapeDtypeStruct((rows_total, count), f32),
            jax.ShapeDtypeStruct((rows_total, count), f32),
            jax.ShapeDtypeStruct((rows_total, 1), f32),
        ),
        in_specs=[whole()] * 3,
        out_specs=[whole()] * 4,
        compiler_params=pltpu.CompilerParams(vmem_limit_bytes=VMEM_BYTES),
        name="encode",
    )(rows, weight, enc_bias.reshape(1, count))


def keep_kernel(latents_ref, sharp_ref, weight_ref, norms_ref, mine_ref, gate_ref, pull_ref):
    rows_total = latents_ref.shape[0]
    half = weight_ref.shape[1] // 2
    latents = latents_ref[...]
    here, _ = core_columns(half)
    mine_ref[...] = jnp.dot(
        latents.astype(jnp.bfloat16), weight_ref[:, here], preferred_element_type=jnp.float32
    )
    gate_ref[...] = jax.nn.sigmoid(sharp_ref[...])
    counts = jnp.sum(latents, axis=0, keepdims=True)
    pull_ref[...] = SPARSITY / (rows_total // 2) * counts / norms_ref[...]


def keep(latents, sharp, weight, norms):
    rows_total, count = latents.shape
    width = weight.shape[1]
    f32 = jnp.float32
    return pl.pallas_call(
        keep_kernel,
        out_shape=(
            jax.ShapeDtypeStruct((rows_total, width // 2), f32),
            jax.ShapeDtypeStruct((rows_total, count), f32),
            jax.ShapeDtypeStruct((1, count), f32),
        ),
        in_specs=[whole()] * 4,
        out_specs=[whole()] * 3,
        compiler_params=pltpu.CompilerParams(vmem_limit_bytes=VMEM_BYTES),
        cost_estimate=pl.CostEstimate(
            flops=rows_total * count * width, bytes_accessed=count * width, transcendentals=0
        ),
        name="keep",
    )(latents, sharp, weight, norms)


def early_kernel(grad_ref, weight_ref, norms_ref, out_ref):
    here, _ = core_columns(weight_ref.shape[1] // 2)
    batch_rows = grad_ref.shape[0] // 2
    out_ref[...] = (
        lax.dot_general(
            grad_ref[...], weight_ref[:, here], NT, preferred_element_type=jnp.float32
        )
        + SPARSITY / batch_rows * norms_ref[...]
    )


def early(grad_mine, weight, norms):
    rows_total, half = grad_mine.shape
    count = weight.shape[0]
    return pl.pallas_call(
        early_kernel,
        out_shape=jax.ShapeDtypeStruct((rows_total, count), jnp.float32),
        in_specs=[whole()] * 3,
        out_specs=whole(),
        compiler_params=pltpu.CompilerParams(vmem_limit_bytes=VMEM_BYTES),
        cost_estimate=pl.CostEstimate(
            flops=2 * rows_total * count * half, bytes_accessed=count * half, transcendentals=0
        ),
        name="early",
    )(grad_mine, weight, norms)


def finish_kernel(
    tile,
    span,
    grad_ref,
    early_ref,
    rows_ref,
    weight_ref,
    latents_ref,
    gate_ref,
    scales_ref,
    pull_ref,
    weight_grad_hbm,
    bias_grad_hbm,
    dec_grad_hbm,
    staged_ref,
    bias_ref,
    dec_ref,
    sums_ref,
    left_ref,
    sems,
):
    rows_total, width = rows_ref.shape
    shares = dec_grad_hbm.shape[0]
    count = width // tile
    core = lax.axis_index("latent")
    _, there = core_columns(width // 2)
    grad_latents = early_ref[...] + lax.dot_general(
        grad_ref[:, there], weight_ref[:, there], NT, preferred_element_type=jnp.float32
    )
    grad_pre = grad_latents * gate_ref[...]
    bias_ref[...] = jnp.sum(grad_pre, axis=0, keepdims=True)
    bias_copy = pltpu.make_async_copy(bias_ref, bias_grad_hbm, sems.at[count])
    bias_copy.start()
    left = jnp.concatenate([grad_pre * scales_ref[...], latents_ref[...]], axis=0)
    left_ref[...] = left.T.astype(jnp.bfloat16)

    sums = jnp.sum(grad_ref[...].astype(jnp.float32), axis=0, keepdims=True)
    sums_ref[:, :width] = jnp.broadcast_to(sums, (8, width))
    sums_ref[:, width:] = jnp.zeros((8, span), jnp.float32)
    offset = lax.axis_index(("dp", "latent")) * shares
    lead = lax.rem(offset, 128)
    window = sums_ref[:, pl.ds(pl.multiple_of(offset - lead, 128), span)]
    window = pltpu.roll(window, lax.rem(span - lead, span), 1)
    dec_ref[...] = window[0, :shares]
    dec_copy = pltpu.make_async_copy(dec_ref, dec_grad_hbm, sems.at[count + 1])
    dec_copy.start()

    copies = [
        pltpu.make_async_copy(
            staged_ref.at[:, pl.ds(index * tile, tile)],
            weight_grad_hbm.at[:, pl.ds(index * tile, tile)],
            sems.at[index],
        )
        for index in range(count)
    ]

    @pl.loop(0, 1 + core // 2)
    def _(_):
        pull = pull_ref[...]
        for index in range(count):
            columns = slice(index * tile, (index + 1) * tile)
            right = jnp.concatenate([rows_ref[:, columns], grad_ref[:, columns]], axis=0)
            total = jnp.dot(left_ref[...], right, preferred_element_type=jnp.float32)
            total = total + pull * weight_ref[:, columns].astype(jnp.float32)
            staged_ref[:, columns] = total.astype(jnp.bfloat16)
            copies[index].start()

    for copy in copies:
        copy.wait()
    bias_copy.wait()
    dec_copy.wait()


def finish(grad_out, early_sum, rows, weight, latents, gate, scales, pull, shares):
    rows_total, width = rows.shape
    count = weight.shape[0]
    tile = 768
    span = (shares + 127 + 127) // 128 * 128
    f32 = jnp.float32
    return pl.pallas_call(
        functools.partial(finish_kernel, tile, span),
        out_shape=(
            jax.ShapeDtypeStruct((count, width), jnp.bfloat16),
            jax.ShapeDtypeStruct((1, count), f32),
            jax.ShapeDtypeStruct((shares,), f32),
        ),
        in_specs=[whole()] * 8,
        out_specs=[whole(pl.ANY)] * 3,
        scratch_shapes=[
            pltpu.VMEM((count, width), jnp.bfloat16),
            pltpu.VMEM((1, count), f32),
            pltpu.VMEM((shares,), f32),
            pltpu.VMEM((8, width + span), f32),
            pltpu.VMEM((count, 2 * rows_total), jnp.bfloat16),
            pltpu.SemaphoreType.DMA((width // tile + 2,)),
        ],
        compiler_params=pltpu.CompilerParams(vmem_limit_bytes=VMEM_BYTES),
        name="finish",
    )(grad_out, early_sum, rows, weight, latents, gate, scales, pull)


def per_device(cur_rows, cached_rows, shuffle_perm, weight, enc_bias, dec_bias):
    dp = lax.axis_size("dp")
    own, width = cur_rows.shape
    columns = cached_rows.shape[1]
    half = width // 2
    count = weight.shape[0]
    batch_rows = dp * own // 2
    core = lax.axis_index("latent")

    arrived = lax.all_to_all(pack(cur_rows, cached_rows, shuffle_perm, dp), "dp", 0, 0)
    gathered = arrived[:, :, :width].reshape(dp * own, width)
    next_batch = arrived[:, :, width:].transpose(1, 0, 2).reshape(own, dp * columns)

    weight_f = weight.astype(jnp.float32)
    norms = jnp.sqrt(jnp.sum(weight_f * weight_f, axis=1) + 1e-06).reshape(1, count)
    send, latents, sharp, scales = encode(gathered, weight, enc_bias)
    came = exchange(send, "latent", 1)
    mine, gate, pull = keep(latents, sharp, weight, norms)

    total = mine + came.astype(jnp.float32)
    corner = min(4, dp)
    sent = total.astype(jnp.bfloat16)
    for distance in range(1, corner):
        total = total + exchange(sent, "dp", distance).astype(jnp.float32)
    distance = corner
    while distance < dp:
        total = total + exchange(total.astype(jnp.bfloat16), "dp", distance).astype(jnp.float32)
        distance *= 2

    target = lax.dynamic_slice_in_dim(gathered, core * half, half, 1).astype(jnp.float32)
    bias = lax.dynamic_slice_in_dim(dec_bias, core * half, half, 0)
    error = total + bias[None, :] - target * scales
    grad_mine = (2.0 / batch_rows * error).astype(jnp.bfloat16)
    grad_other = exchange(grad_mine, "latent", 1)
    early_sum = early(grad_mine, weight, norms)
    low = jnp.where(core == 0, grad_mine, grad_other)
    high = jnp.where(core == 0, grad_other, grad_mine)
    grad_out = jnp.concatenate([low, high], axis=1)

    shares = width // (2 * dp)
    weight_grad, enc_bias_grad, dec_bias_grad = finish(
        grad_out,
        early_sum,
        gathered,
        weight,
        latents,
        gate,
        scales,
        pull.reshape(count, 1),
        shares,
    )
    return (weight_grad, enc_bias_grad.reshape(count), dec_bias_grad, next_batch)


def solution(mesh):
    return jax.shard_map(
        per_device,
        mesh=mesh,
        in_specs=(
            P(("group", "dp"), None),
            P("group", "dp"),
            P("group"),
            P(("group", "dp", "latent"), None),
            P(("group", "dp", "latent")),
            P("group"),
        ),
        out_specs=(
            P(("group", "dp", "latent"), None),
            P(("group", "dp", "latent")),
            P(("group", "dp", "latent")),
            P(("group", "dp"), None),
        ),
        check_vma=False,
    )
```

```python
import functools

import jax
import jax.numpy as jnp
from jax import lax
from jax.experimental import pallas as pl
from jax.experimental.pallas import tpu as pltpu
from jax.sharding import PartitionSpec as P

SPARSITY = 4.0
SHARP = 4.0
VMEM_BYTES = 16 * 1024 * 1024
PACK_BYTES = 60 * 1024 * 1024
NT = (((1,), (1,)), ((), ()))
TN = (((0,), (0,)), ((), ()))


def whole(space=pltpu.VMEM):
    return pl.BlockSpec(memory_space=space)


def exchange(value, axis, distance):
    size = lax.axis_size(axis)
    return lax.ppermute(value, axis, [(k, k ^ distance) for k in range(size)])


def core_columns(half):
    core = lax.axis_index("latent")
    here = pl.ds(pl.multiple_of(core * half, 128), half)
    there = pl.ds(pl.multiple_of((1 - core) * half, 128), half)
    return here, there


def pack_kernel(
    cur_hbm, cached_hbm, perm_hbm, out_hbm, cur_ref, cached_ref, perm_ref, staged_ref, sems
):
    dp, own, _ = out_hbm.shape
    width = cur_hbm.shape[1]
    row_total, columns = cached_ref.shape
    fetches = [
        pltpu.make_async_copy(source, target, sems.at[index])
        for index, (source, target) in enumerate(
            [(cur_hbm, cur_ref), (cached_hbm, cached_ref), (perm_hbm, perm_ref)]
        )
    ]
    for fetch in fetches:
        fetch.start()
    rows_copy, next_copy = (
        pltpu.make_async_copy(staged_ref.at[:, :, part], out_hbm.at[:, :, part], sem)
        for part, sem in (
            (pl.ds(0, width), sems.at[3]),
            (pl.ds(width, columns), sems.at[4]),
        )
    )
    fetches[0].wait()
    cur = cur_ref[...]
    for peer in range(dp):
        staged_ref[peer, :, :width] = cur
    rows_copy.start()
    fetches[1].wait()
    fetches[2].wait()
    slots = lax.broadcasted_iota(jnp.int32, (row_total, row_total), 0)
    selector = (jnp.broadcast_to(perm_ref[...], slots.shape) == slots).astype(jnp.bfloat16)
    ordered = jnp.dot(selector, cached_ref[...], preferred_element_type=jnp.float32)
    for peer in range(dp):
        staged_ref[peer, :, width:] = ordered[peer * own : (peer + 1) * own].astype(jnp.bfloat16)
    next_copy.start()
    rows_copy.wait()
    next_copy.wait()


def pack(cur_rows, cached_rows, shuffle_perm, dp):
    own, width = cur_rows.shape
    row_total, columns = cached_rows.shape
    return pl.pallas_call(
        pack_kernel,
        out_shape=jax.ShapeDtypeStruct((dp, own, width + columns), jnp.bfloat16),
        in_specs=[whole(pl.ANY)] * 3,
        out_specs=whole(pl.ANY),
        scratch_shapes=[
            pltpu.VMEM((own, width), jnp.bfloat16),
            pltpu.VMEM((row_total, columns), jnp.bfloat16),
            pltpu.VMEM((1, row_total), jnp.int32),
            pltpu.VMEM((dp, own, width + columns), jnp.bfloat16),
            pltpu.SemaphoreType.DMA((5,)),
        ],
        compiler_params=pltpu.CompilerParams(vmem_limit_bytes=PACK_BYTES),
        name="pack",
    )(cur_rows, cached_rows, shuffle_perm.reshape(1, row_total))


def encode_kernel(rows_ref, weight_ref, bias_ref, send_ref, latents_ref, sharp_ref, scales_ref):
    rows_total, width = rows_ref.shape
    batch_rows = rows_total // 2
    projected = lax.dot_general(
        rows_ref[...], weight_ref[...], NT, preferred_element_type=jnp.float32
    )
    rows_f = rows_ref[...].astype(jnp.float32)
    squares = jnp.sum(rows_f * rows_f, axis=1, keepdims=True)
    first = jnp.sum(squares[:batch_rows], axis=0, keepdims=True) / batch_rows
    second = jnp.sum(squares[batch_rows:], axis=0, keepdims=True) / batch_rows
    row = lax.broadcasted_iota(jnp.int32, (rows_total, 1), 0)
    scales = jnp.sqrt(width / jnp.where(row < batch_rows, first, second))
    scales_ref[...] = scales
    sharp = SHARP * (scales * projected + bias_ref[...])
    latents = jax.nn.softplus(sharp) / SHARP
    sharp_ref[...] = sharp
    latents_ref[...] = latents
    _, there = core_columns(width // 2)
    send_ref[...] = jnp.dot(
        latents.astype(jnp.bfloat16), weight_ref[:, there], preferred_element_type=jnp.float32
    ).astype(jnp.bfloat16)


def encode(rows, weight, enc_bias):
    rows_total, width = rows.shape
    count = weight.shape[0]
    f32 = jnp.float32
    return pl.pallas_call(
        encode_kernel,
        out_shape=(
            jax.ShapeDtypeStruct((rows_total, width // 2), jnp.bfloat16),
            jax.ShapeDtypeStruct((rows_total, count), f32),
            jax.ShapeDtypeStruct((rows_total, count), f32),
            jax.ShapeDtypeStruct((rows_total, 1), f32),
        ),
        in_specs=[whole()] * 3,
        out_specs=[whole()] * 4,
        compiler_params=pltpu.CompilerParams(vmem_limit_bytes=VMEM_BYTES),
        name="encode",
    )(rows, weight, enc_bias.reshape(1, count))


def keep_kernel(latents_ref, sharp_ref, weight_ref, norms_ref, mine_ref, gate_ref, pull_ref):
    rows_total = latents_ref.shape[0]
    half = weight_ref.shape[1] // 2
    latents = latents_ref[...]
    here, _ = core_columns(half)
    mine_ref[...] = jnp.dot(
        latents.astype(jnp.bfloat16), weight_ref[:, here], preferred_element_type=jnp.float32
    )
    gate_ref[...] = jax.nn.sigmoid(sharp_ref[...])
    counts = jnp.sum(latents, axis=0, keepdims=True)
    pull_ref[...] = SPARSITY / (rows_total // 2) * counts / norms_ref[...]


def keep(latents, sharp, weight, norms):
    rows_total, count = latents.shape
    width = weight.shape[1]
    f32 = jnp.float32
    return pl.pallas_call(
        keep_kernel,
        out_shape=(
            jax.ShapeDtypeStruct((rows_total, width // 2), f32),
            jax.ShapeDtypeStruct((rows_total, count), f32),
            jax.ShapeDtypeStruct((1, count), f32),
        ),
        in_specs=[whole()] * 4,
        out_specs=[whole()] * 3,
        compiler_params=pltpu.CompilerParams(vmem_limit_bytes=VMEM_BYTES),
        cost_estimate=pl.CostEstimate(
            flops=rows_total * count * width, bytes_accessed=count * width, transcendentals=0
        ),
        name="keep",
    )(latents, sharp, weight, norms)


def early_kernel(grad_ref, weight_ref, norms_ref, out_ref):
    here, _ = core_columns(weight_ref.shape[1] // 2)
    batch_rows = grad_ref.shape[0] // 2
    out_ref[...] = (
        lax.dot_general(
            grad_ref[...], weight_ref[:, here], NT, preferred_element_type=jnp.float32
        )
        + SPARSITY / batch_rows * norms_ref[...]
    )


def early(grad_mine, weight, norms):
    rows_total, half = grad_mine.shape
    count = weight.shape[0]
    return pl.pallas_call(
        early_kernel,
        out_shape=jax.ShapeDtypeStruct((rows_total, count), jnp.float32),
        in_specs=[whole()] * 3,
        out_specs=whole(),
        compiler_params=pltpu.CompilerParams(vmem_limit_bytes=VMEM_BYTES),
        cost_estimate=pl.CostEstimate(
            flops=2 * rows_total * count * half, bytes_accessed=count * half, transcendentals=0
        ),
        name="early",
    )(grad_mine, weight, norms)


def finish_kernel(
    tile,
    span,
    grad_ref,
    early_ref,
    rows_ref,
    weight_ref,
    latents_ref,
    gate_ref,
    scales_ref,
    pull_ref,
    weight_grad_hbm,
    bias_grad_hbm,
    dec_grad_hbm,
    staged_ref,
    bias_ref,
    dec_ref,
    sums_ref,
    left_ref,
    sems,
):
    rows_total, width = rows_ref.shape
    shares = dec_grad_hbm.shape[0]
    count = width // tile
    core = lax.axis_index("latent")
    _, there = core_columns(width // 2)
    grad_latents = early_ref[...] + lax.dot_general(
        grad_ref[:, there], weight_ref[:, there], NT, preferred_element_type=jnp.float32
    )
    grad_pre = grad_latents * gate_ref[...]
    bias_ref[...] = jnp.sum(grad_pre, axis=0, keepdims=True)
    bias_copy = pltpu.make_async_copy(bias_ref, bias_grad_hbm, sems.at[count])
    bias_copy.start()
    left = jnp.concatenate([grad_pre * scales_ref[...], latents_ref[...]], axis=0)
    left_ref[...] = left.T.astype(jnp.bfloat16)

    sums = jnp.sum(grad_ref[...].astype(jnp.float32), axis=0, keepdims=True)
    sums_ref[:, :width] = jnp.broadcast_to(sums, (8, width))
    sums_ref[:, width:] = jnp.zeros((8, span), jnp.float32)
    offset = lax.axis_index(("dp", "latent")) * shares
    lead = lax.rem(offset, 128)
    window = sums_ref[:, pl.ds(pl.multiple_of(offset - lead, 128), span)]
    window = pltpu.roll(window, lax.rem(span - lead, span), 1)
    dec_ref[...] = window[0, :shares]
    dec_copy = pltpu.make_async_copy(dec_ref, dec_grad_hbm, sems.at[count + 1])
    dec_copy.start()

    copies = [
        pltpu.make_async_copy(
            staged_ref.at[:, pl.ds(index * tile, tile)],
            weight_grad_hbm.at[:, pl.ds(index * tile, tile)],
            sems.at[index],
        )
        for index in range(count)
    ]

    @pl.loop(0, 1 + core // 2)
    def _(_):
        pull = pull_ref[...]
        for index in range(count):
            columns = slice(index * tile, (index + 1) * tile)
            right = jnp.concatenate([rows_ref[:, columns], grad_ref[:, columns]], axis=0)
            total = jnp.dot(left_ref[...], right, preferred_element_type=jnp.float32)
            total = total + pull * weight_ref[:, columns].astype(jnp.float32)
            staged_ref[:, columns] = total.astype(jnp.bfloat16)
            copies[index].start()

    for copy in copies:
        copy.wait()
    bias_copy.wait()
    dec_copy.wait()


def finish(grad_out, early_sum, rows, weight, latents, gate, scales, pull, shares):
    rows_total, width = rows.shape
    count = weight.shape[0]
    tile = 768
    span = (shares + 127 + 127) // 128 * 128
    f32 = jnp.float32
    return pl.pallas_call(
        functools.partial(finish_kernel, tile, span),
        out_shape=(
            jax.ShapeDtypeStruct((count, width), jnp.bfloat16),
            jax.ShapeDtypeStruct((1, count), f32),
            jax.ShapeDtypeStruct((shares,), f32),
        ),
        in_specs=[whole()] * 8,
        out_specs=[whole(pl.ANY)] * 3,
        scratch_shapes=[
            pltpu.VMEM((count, width), jnp.bfloat16),
            pltpu.VMEM((1, count), f32),
            pltpu.VMEM((shares,), f32),
            pltpu.VMEM((8, width + span), f32),
            pltpu.VMEM((count, 2 * rows_total), jnp.bfloat16),
            pltpu.SemaphoreType.DMA((width // tile + 2,)),
        ],
        compiler_params=pltpu.CompilerParams(vmem_limit_bytes=VMEM_BYTES),
        name="finish",
    )(grad_out, early_sum, rows, weight, latents, gate, scales, pull)


def per_device(cur_rows, cached_rows, shuffle_perm, weight, enc_bias, dec_bias):
    dp = lax.axis_size("dp")
    own, width = cur_rows.shape
    columns = cached_rows.shape[1]
    half = width // 2
    count = weight.shape[0]
    batch_rows = dp * own // 2
    core = lax.axis_index("latent")

    arrived = lax.all_to_all(pack(cur_rows, cached_rows, shuffle_perm, dp), "dp", 0, 0)
    gathered = arrived[:, :, :width].reshape(dp * own, width)
    next_batch = arrived[:, :, width:].transpose(1, 0, 2).reshape(own, dp * columns)

    weight_f = weight.astype(jnp.float32)
    norms = jnp.sqrt(jnp.sum(weight_f * weight_f, axis=1) + 1e-06).reshape(1, count)
    send, latents, sharp, scales = encode(gathered, weight, enc_bias)
    came = exchange(send, "latent", 1)
    mine, gate, pull = keep(latents, sharp, weight, norms)

    total = mine + came.astype(jnp.float32)
    corner = min(4, dp)
    sent = total.astype(jnp.bfloat16)
    for distance in range(1, corner):
        total = total + exchange(sent, "dp", distance).astype(jnp.float32)
    distance = corner
    while distance < dp:
        total = total + exchange(total.astype(jnp.bfloat16), "dp", distance).astype(jnp.float32)
        distance *= 2

    target = lax.dynamic_slice_in_dim(gathered, core * half, half, 1).astype(jnp.float32)
    bias = lax.dynamic_slice_in_dim(dec_bias, core * half, half, 0)
    error = total + bias[None, :] - target * scales
    grad_mine = (2.0 / batch_rows * error).astype(jnp.bfloat16)
    grad_other = exchange(grad_mine, "latent", 1)
    early_sum = early(grad_mine, weight, norms)
    low = jnp.where(core == 0, grad_mine, grad_other)
    high = jnp.where(core == 0, grad_other, grad_mine)
    grad_out = jnp.concatenate([low, high], axis=1)

    shares = width // (2 * dp)
    weight_grad, enc_bias_grad, dec_bias_grad = finish(
        grad_out,
        early_sum,
        gathered,
        weight,
        latents,
        gate,
        scales,
        pull.reshape(count, 1),
        shares,
    )
    return (weight_grad, enc_bias_grad.reshape(count), dec_bias_grad, next_batch)


def solution(mesh):
    return jax.shard_map(
        per_device,
        mesh=mesh,
        in_specs=(
            P(("group", "dp"), None),
            P("group", "dp"),
            P("group"),
            P(("group", "dp", "latent"), None),
            P(("group", "dp", "latent")),
            P("group"),
        ),
        out_specs=(
            P(("group", "dp", "latent"), None),
            P(("group", "dp", "latent")),
            P(("group", "dp", "latent")),
            P(("group", "dp"), None),
        ),
        check_vma=False,
    )
```

```python
import functools

import jax
import jax.numpy as jnp
from jax import lax
from jax.experimental import pallas as pl
from jax.experimental.pallas import tpu as pltpu
from jax.sharding import PartitionSpec as P

SPARSITY = 4.0
SHARP = 4.0
VMEM_BYTES = 16 * 1024 * 1024
NT = (((1,), (1,)), ((), ()))
TN = (((0,), (0,)), ((), ()))


def whole(space=pltpu.VMEM):
    return pl.BlockSpec(memory_space=space)


def exchange(value, axis, distance):
    size = lax.axis_size(axis)
    return lax.ppermute(value, axis, [(k, k ^ distance) for k in range(size)])


def core_columns(half):
    core = lax.axis_index("latent")
    here = pl.ds(pl.multiple_of(core * half, 128), half)
    there = pl.ds(pl.multiple_of((1 - core) * half, 128), half)
    return here, there


def flip_rows(value, distance):
    count = value.shape[0]
    row = lax.broadcasted_iota(jnp.int32, value.shape, 0)
    bit = 1
    while bit <= distance:
        if distance & bit:
            up = pltpu.roll(value, count - bit, 0)
            down = pltpu.roll(value, bit, 0)
            value = jnp.where(row & bit == 0, up, down)
        bit *= 2
    return value


def order_kernel(own, cached_hbm, perm_hbm, out_ref, cached_ref, perm_ref, sems):
    row_total, columns = cached_ref.shape
    dp = row_total // own
    fetches = [
        pltpu.make_async_copy(cached_hbm, cached_ref, sems.at[0]),
        pltpu.make_async_copy(perm_hbm, perm_ref, sems.at[1]),
    ]
    for fetch in fetches:
        fetch.start()
    row = lax.broadcasted_iota(jnp.int32, (row_total, row_total), 0)
    rest = dp // 4
    distance = row // (rest * own) + 4 * (row // own % rest)
    wanted = (distance ^ lax.axis_index("dp")) * own + row % own
    for fetch in fetches:
        fetch.wait()
    selector = (jnp.broadcast_to(perm_ref[...], row.shape) == wanted).astype(jnp.bfloat16)
    out_ref[...] = jnp.dot(
        selector, cached_ref[...], preferred_element_type=jnp.float32
    ).astype(jnp.bfloat16)


def order(cached_rows, shuffle_perm, own):
    row_total, columns = cached_rows.shape
    return pl.pallas_call(
        functools.partial(order_kernel, own),
        out_shape=jax.ShapeDtypeStruct((row_total, columns), jnp.bfloat16),
        in_specs=[whole(pl.ANY)] * 2,
        out_specs=whole(),
        scratch_shapes=[
            pltpu.VMEM((row_total, columns), jnp.bfloat16),
            pltpu.VMEM((1, row_total), jnp.int32),
            pltpu.SemaphoreType.DMA((2,)),
        ],
        compiler_params=pltpu.CompilerParams(vmem_limit_bytes=VMEM_BYTES),
        cost_estimate=pl.CostEstimate(flops=4000000, bytes_accessed=2000000, transcendentals=0),
        name="order",
    )(cached_rows, shuffle_perm.reshape(1, row_total))


def encode_kernel(
    own,
    first_ref,
    second_ref,
    third_ref,
    fourth_ref,
    weight_ref,
    bias_ref,
    send_ref,
    rows_ref,
    latents_ref,
    sharp_ref,
    scales_ref,
    rows_f_ref,
):
    rows_total, width = rows_f_ref.shape
    batch_rows = rows_total // 2
    part = rows_total // 4
    for index, ref in enumerate((first_ref, second_ref, third_ref, fourth_ref)):
        value = ref[...].astype(jnp.float32)
        rows_f_ref[index * part : (index + 1) * part] = value[:, :width]
    rows_f = rows_f_ref[...]
    rows = rows_f.astype(jnp.bfloat16)
    rows_ref[...] = rows
    projected = lax.dot_general(rows, weight_ref[...], NT, preferred_element_type=jnp.float32)
    squares = jnp.sum(rows_f * rows_f, axis=1, keepdims=True)
    row = lax.broadcasted_iota(jnp.int32, (rows_total, 1), 0)
    rest = part // own
    near = row // own % rest < rest // 2
    here = jnp.sum(jnp.where(near, squares, 0.0), axis=0, keepdims=True) / batch_rows
    far = jnp.sum(jnp.where(near, 0.0, squares), axis=0, keepdims=True) / batch_rows
    scales = jnp.sqrt(width / jnp.where(near, here, far))
    scales_ref[...] = scales
    sharp = SHARP * (scales * projected + bias_ref[...])
    latents = jax.nn.softplus(sharp) / SHARP
    sharp_ref[...] = sharp
    latents_ref[...] = latents
    _, there = core_columns(width // 2)
    send_ref[...] = jnp.dot(
        latents.astype(jnp.bfloat16), weight_ref[:, there], preferred_element_type=jnp.float32
    ).astype(jnp.bfloat16)


def encode(parts, weight, enc_bias, own):
    count, width = weight.shape
    rows_total = 4 * parts[0].shape[0]
    f32 = jnp.float32
    return pl.pallas_call(
        functools.partial(encode_kernel, own),
        out_shape=(
            jax.ShapeDtypeStruct((rows_total, width // 2), jnp.bfloat16),
            jax.ShapeDtypeStruct((rows_total, width), jnp.bfloat16),
            jax.ShapeDtypeStruct((rows_total, count), f32),
            jax.ShapeDtypeStruct((rows_total, count), f32),
            jax.ShapeDtypeStruct((rows_total, 1), f32),
        ),
        in_specs=[whole()] * 6,
        out_specs=[whole()] * 5,
        scratch_shapes=[pltpu.VMEM((rows_total, width), f32)],
        compiler_params=pltpu.CompilerParams(vmem_limit_bytes=VMEM_BYTES),
        name="encode",
    )(*parts, weight, enc_bias.reshape(1, count))


def keep_kernel(latents_ref, sharp_ref, weight_ref, norms_ref, mine_ref, gate_ref, pull_ref):
    rows_total = latents_ref.shape[0]
    half = weight_ref.shape[1] // 2
    latents = latents_ref[...]
    here, _ = core_columns(half)
    mine_ref[...] = jnp.dot(
        latents.astype(jnp.bfloat16), weight_ref[:, here], preferred_element_type=jnp.float32
    )
    gate_ref[...] = jax.nn.sigmoid(sharp_ref[...])
    counts = jnp.sum(latents, axis=0, keepdims=True)
    pull_ref[...] = SPARSITY / (rows_total // 2) * counts / norms_ref[...]


def keep(latents, sharp, weight, norms):
    rows_total, count = latents.shape
    width = weight.shape[1]
    f32 = jnp.float32
    return pl.pallas_call(
        keep_kernel,
        out_shape=(
            jax.ShapeDtypeStruct((rows_total, width // 2), f32),
            jax.ShapeDtypeStruct((rows_total, count), f32),
            jax.ShapeDtypeStruct((1, count), f32),
        ),
        in_specs=[whole()] * 4,
        out_specs=[whole()] * 3,
        compiler_params=pltpu.CompilerParams(vmem_limit_bytes=VMEM_BYTES),
        cost_estimate=pl.CostEstimate(
            flops=rows_total * count * width, bytes_accessed=count * width, transcendentals=0
        ),
        name="keep",
    )(latents, sharp, weight, norms)


def merge_kernel(distances, total_ref, *refs):
    total = total_ref[...]
    for distance, ref in zip(distances, refs):
        total = total + flip_rows(ref[...].astype(jnp.float32), distance)
    sum_ref, sent_ref = refs[len(distances) :]
    sum_ref[...] = total
    sent_ref[...] = total.astype(jnp.bfloat16)


def merge(total, arrived, distances):
    return pl.pallas_call(
        functools.partial(merge_kernel, distances),
        out_shape=(
            jax.ShapeDtypeStruct(total.shape, jnp.float32),
            jax.ShapeDtypeStruct(total.shape, jnp.bfloat16),
        ),
        in_specs=[whole()] * (1 + len(arrived)),
        out_specs=[whole()] * 2,
        compiler_params=pltpu.CompilerParams(vmem_limit_bytes=VMEM_BYTES),
        name="merge",
    )(total, *arrived)


def settle_kernel(distance, total_ref, arrived_ref, rows_ref, scales_ref, bias_ref, grad_ref):
    rows_total, width = rows_ref.shape
    here, _ = core_columns(width // 2)
    total = total_ref[...] + flip_rows(arrived_ref[...].astype(jnp.float32), distance)
    target = rows_ref[:, here].astype(jnp.float32) * scales_ref[...]
    error = total + bias_ref[:, here] - target
    grad_ref[...] = (2.0 / (rows_total // 2) * error).astype(jnp.bfloat16)


def settle(total, arrived, rows, scales, dec_bias, distance):
    return pl.pallas_call(
        functools.partial(settle_kernel, distance),
        out_shape=jax.ShapeDtypeStruct(total.shape, jnp.bfloat16),
        in_specs=[whole()] * 5,
        out_specs=whole(),
        compiler_params=pltpu.CompilerParams(vmem_limit_bytes=VMEM_BYTES),
        name="settle",
    )(total, arrived, rows, scales, dec_bias.reshape(1, -1))


def early_kernel(grad_ref, weight_ref, norms_ref, out_ref):
    here, _ = core_columns(weight_ref.shape[1] // 2)
    batch_rows = grad_ref.shape[0] // 2
    out_ref[...] = (
        lax.dot_general(
            grad_ref[...], weight_ref[:, here], NT, preferred_element_type=jnp.float32
        )
        + SPARSITY / batch_rows * norms_ref[...]
    )


def early(grad_mine, weight, norms):
    rows_total, half = grad_mine.shape
    count = weight.shape[0]
    return pl.pallas_call(
        early_kernel,
        out_shape=jax.ShapeDtypeStruct((rows_total, count), jnp.float32),
        in_specs=[whole()] * 3,
        out_specs=whole(),
        compiler_params=pltpu.CompilerParams(vmem_limit_bytes=VMEM_BYTES),
        cost_estimate=pl.CostEstimate(
            flops=2 * rows_total * count * half, bytes_accessed=count * half, transcendentals=0
        ),
        name="early",
    )(grad_mine, weight, norms)


def finish_kernel(
    tile,
    span,
    grad_ref,
    early_ref,
    rows_ref,
    weight_ref,
    latents_ref,
    gate_ref,
    scales_ref,
    pull_ref,
    weight_grad_hbm,
    bias_grad_hbm,
    dec_grad_hbm,
    staged_ref,
    bias_ref,
    dec_ref,
    sums_ref,
    left_ref,
    sems,
):
    rows_total, width = rows_ref.shape
    shares = dec_grad_hbm.shape[0]
    count = width // tile
    core = lax.axis_index("latent")
    _, there = core_columns(width // 2)
    grad_latents = early_ref[...] + lax.dot_general(
        grad_ref[:, there], weight_ref[:, there], NT, preferred_element_type=jnp.float32
    )
    grad_pre = grad_latents * gate_ref[...]
    bias_ref[...] = jnp.sum(grad_pre, axis=0, keepdims=True)
    bias_copy = pltpu.make_async_copy(bias_ref, bias_grad_hbm, sems.at[count])
    bias_copy.start()
    left = jnp.concatenate([grad_pre * scales_ref[...], latents_ref[...]], axis=0)
    left_ref[...] = left.T.astype(jnp.bfloat16)

    sums = jnp.sum(grad_ref[...].astype(jnp.float32), axis=0, keepdims=True)
    sums_ref[:, :width] = jnp.broadcast_to(sums, (8, width))
    sums_ref[:, width:] = jnp.zeros((8, span), jnp.float32)
    offset = lax.axis_index(("dp", "latent")) * shares
    lead = lax.rem(offset, 128)
    window = sums_ref[:, pl.ds(pl.multiple_of(offset - lead, 128), span)]
    window = pltpu.roll(window, lax.rem(span - lead, span), 1)
    dec_ref[...] = window[0, :shares]
    dec_copy = pltpu.make_async_copy(dec_ref, dec_grad_hbm, sems.at[count + 1])
    dec_copy.start()

    copies = [
        pltpu.make_async_copy(
            staged_ref.at[:, pl.ds(index * tile, tile)],
            weight_grad_hbm.at[:, pl.ds(index * tile, tile)],
            sems.at[index],
        )
        for index in range(count)
    ]

    @pl.loop(0, 1 + core // 2)
    def _(_):
        pull = pull_ref[...]
        for index in range(count):
            columns = slice(index * tile, (index + 1) * tile)
            right = jnp.concatenate([rows_ref[:, columns], grad_ref[:, columns]], axis=0)
            total = jnp.dot(left_ref[...], right, preferred_element_type=jnp.float32)
            total = total + pull * weight_ref[:, columns].astype(jnp.float32)
            staged_ref[:, columns] = total.astype(jnp.bfloat16)
            copies[index].start()

    for copy in copies:
        copy.wait()
    bias_copy.wait()
    dec_copy.wait()


def finish(grad_out, early_sum, rows, weight, latents, gate, scales, pull, shares):
    rows_total, width = rows.shape
    count = weight.shape[0]
    tile = 768
    span = (shares + 127 + 127) // 128 * 128
    f32 = jnp.float32
    return pl.pallas_call(
        functools.partial(finish_kernel, tile, span),
        out_shape=(
            jax.ShapeDtypeStruct((count, width), jnp.bfloat16),
            jax.ShapeDtypeStruct((1, count), f32),
            jax.ShapeDtypeStruct((shares,), f32),
        ),
        in_specs=[whole()] * 8,
        out_specs=[whole(pl.ANY)] * 3,
        scratch_shapes=[
            pltpu.VMEM((count, width), jnp.bfloat16),
            pltpu.VMEM((1, count), f32),
            pltpu.VMEM((shares,), f32),
            pltpu.VMEM((8, width + span), f32),
            pltpu.VMEM((count, 2 * rows_total), jnp.bfloat16),
            pltpu.SemaphoreType.DMA((width // tile + 2,)),
        ],
        compiler_params=pltpu.CompilerParams(vmem_limit_bytes=VMEM_BYTES),
        name="finish",
    )(grad_out, early_sum, rows, weight, latents, gate, scales, pull)


def per_device(cur_rows, cached_rows, shuffle_perm, weight, enc_bias, dec_bias):
    dp = lax.axis_size("dp")
    rest = dp // 4
    own, width = cur_rows.shape
    columns = cached_rows.shape[1]
    count = weight.shape[0]
    place = lax.axis_index("dp")
    core = lax.axis_index("latent")

    near = cur_rows
    distance = 4
    while distance < dp:
        near = jnp.concatenate([near, exchange(near, "dp", distance)], axis=0)
        distance *= 2
    ordered = order(cached_rows, shuffle_perm, own).reshape(4, rest * own, columns)
    parts = [near] + [
        exchange(jnp.concatenate([near, ordered[low]], axis=1), "dp", low) for low in range(1, 4)
    ]

    weight_f = weight.astype(jnp.float32)
    norms = jnp.sqrt(jnp.sum(weight_f * weight_f, axis=1) + 1e-06).reshape(1, count)
    send, gathered, latents, sharp, scales = encode(parts, weight, enc_bias, own)
    came = exchange(send, "latent", 1)
    mine, gate, pull = keep(latents, sharp, weight, norms)

    total = mine + came.astype(jnp.float32)
    sent = total.astype(jnp.bfloat16)
    lows = (1, 2, 3)
    total, sent = merge(
        total,
        [exchange(sent, "dp", low) for low in lows],
        tuple(low * rest * own for low in lows),
    )

    riders = jnp.stack([ordered[0]] + [part[:, width:] for part in parts[1:]])
    riders = riders.reshape(4, rest, own, columns).transpose(1, 0, 2, 3)
    riders, sent = lax.optimization_barrier((riders, sent))
    distance = 4
    while distance < dp:
        arrived = exchange(sent, "dp", distance)
        split = riders.reshape((-1, 2) + riders.shape[1:])
        riders = jnp.concatenate([split[:, 0], exchange(split[:, 1], "dp", distance)], axis=1)
        row_distance = distance // 4 * own
        if 2 * distance < dp:
            total, sent = merge(total, [arrived], (row_distance,))
        else:
            grad_mine = settle(total, arrived, gathered, scales, dec_bias, row_distance)
        distance *= 2

    riders = riders[0]
    bit = 1
    while bit < dp:
        pairs = riders.reshape(dp // (2 * bit), 2, bit * own * columns)
        pairs = jnp.where(place & bit == 0, pairs, pairs[:, ::-1])
        riders = pairs.reshape(dp, own, columns)
        bit *= 2
    next_batch = riders.transpose(1, 0, 2).reshape(own, dp * columns)

    grad_other = exchange(grad_mine, "latent", 1)
    early_sum = early(grad_mine, weight, norms)
    low_half = jnp.where(core == 0, grad_mine, grad_other)
    high_half = jnp.where(core == 0, grad_other, grad_mine)
    grad_out = jnp.concatenate([low_half, high_half], axis=1)

    shares = width // (2 * dp)
    weight_grad, enc_bias_grad, dec_bias_grad = finish(
        grad_out,
        early_sum,
        gathered,
        weight,
        latents,
        gate,
        scales,
        pull.reshape(count, 1),
        shares,
    )
    return (weight_grad, enc_bias_grad.reshape(count), dec_bias_grad, next_batch)


def solution(mesh):
    return jax.shard_map(
        per_device,
        mesh=mesh,
        in_specs=(
            P(("group", "dp"), None),
            P("group", "dp"),
            P("group"),
            P(("group", "dp", "latent"), None),
            P(("group", "dp", "latent")),
            P("group"),
        ),
        out_specs=(
            P(("group", "dp", "latent"), None),
            P(("group", "dp", "latent")),
            P(("group", "dp", "latent")),
            P(("group", "dp"), None),
        ),
        check_vma=False,
    )
```

```python
import functools

import jax
import jax.numpy as jnp
from jax import lax
from jax.experimental import pallas as pl
from jax.experimental.pallas import tpu as pltpu
from jax.sharding import PartitionSpec as P

SPARSITY = 4.0
SHARP = 4.0
VMEM_BYTES = 16 * 1024 * 1024
NT = (((1,), (1,)), ((), ()))
TN = (((0,), (0,)), ((), ()))


def whole(space=pltpu.VMEM):
    return pl.BlockSpec(memory_space=space)


def exchange(value, axis, distance):
    size = lax.axis_size(axis)
    return lax.ppermute(value, axis, [(k, k ^ distance) for k in range(size)])


def core_columns(half):
    core = lax.axis_index("latent")
    here = pl.ds(pl.multiple_of(core * half, 128), half)
    there = pl.ds(pl.multiple_of((1 - core) * half, 128), half)
    return here, there


def flip_rows(value, distance):
    count = value.shape[0]
    row = lax.broadcasted_iota(jnp.int32, value.shape, 0)
    bit = 1
    while bit <= distance:
        if distance & bit:
            up = pltpu.roll(value, count - bit, 0)
            down = pltpu.roll(value, bit, 0)
            value = jnp.where(row & bit == 0, up, down)
        bit *= 2
    return value


def order_kernel(
    cur_hbm,
    cached_hbm,
    perm_hbm,
    weight_hbm,
    out_ref,
    cur_ref,
    weight_ref,
    cached_ref,
    perm_ref,
    sems,
):
    row_total, columns = cached_ref.shape
    own = cur_ref.shape[0]
    dp = row_total // own
    fetches = [
        pltpu.make_async_copy(cached_hbm, cached_ref, sems.at[0]),
        pltpu.make_async_copy(perm_hbm, perm_ref, sems.at[1]),
        pltpu.make_async_copy(cur_hbm, cur_ref, sems.at[2]),
        pltpu.make_async_copy(weight_hbm, weight_ref, sems.at[3]),
    ]
    for fetch in fetches:
        fetch.start()
    row = lax.broadcasted_iota(jnp.int32, (row_total, row_total), 0)
    rest = dp // 4
    distance = row // (rest * own) + 4 * (row // own % rest)
    wanted = (distance ^ lax.axis_index("dp")) * own + row % own
    for fetch in fetches[:2]:
        fetch.wait()
    selector = (jnp.broadcast_to(perm_ref[...], row.shape) == wanted).astype(jnp.bfloat16)
    out_ref[...] = jnp.dot(
        selector, cached_ref[...], preferred_element_type=jnp.float32
    ).astype(jnp.bfloat16)
    for fetch in fetches[2:]:
        fetch.wait()


def order(cur_rows, cached_rows, shuffle_perm, weight):
    row_total, columns = cached_rows.shape
    return pl.pallas_call(
        order_kernel,
        out_shape=(
            jax.ShapeDtypeStruct((row_total, columns), jnp.bfloat16),
            jax.ShapeDtypeStruct(cur_rows.shape, jnp.bfloat16),
            jax.ShapeDtypeStruct(weight.shape, jnp.bfloat16),
        ),
        in_specs=[whole(pl.ANY)] * 4,
        out_specs=[whole()] * 3,
        scratch_shapes=[
            pltpu.VMEM((row_total, columns), jnp.bfloat16),
            pltpu.VMEM((1, row_total), jnp.int32),
            pltpu.SemaphoreType.DMA((4,)),
        ],
        compiler_params=pltpu.CompilerParams(vmem_limit_bytes=VMEM_BYTES),
        cost_estimate=pl.CostEstimate(flops=4000000, bytes_accessed=2000000, transcendentals=0),
        name="order",
    )(
        *(
            pltpu.with_memory_space_constraint(value, pltpu.MemorySpace.HBM)
            for value in (cur_rows, cached_rows, shuffle_perm.reshape(1, row_total), weight)
        )
    )


def encode_kernel(
    own,
    first_ref,
    second_ref,
    third_ref,
    fourth_ref,
    weight_ref,
    bias_ref,
    send_ref,
    rows_ref,
    latents_ref,
    sharp_ref,
    scales_ref,
    rows_f_ref,
):
    rows_total, width = rows_f_ref.shape
    batch_rows = rows_total // 2
    part = rows_total // 4
    for index, ref in enumerate((first_ref, second_ref, third_ref, fourth_ref)):
        value = ref[...].astype(jnp.float32)
        rows_f_ref[index * part : (index + 1) * part] = value[:, :width]
    rows_f = rows_f_ref[...]
    rows = rows_f.astype(jnp.bfloat16)
    rows_ref[...] = rows
    projected = lax.dot_general(rows, weight_ref[...], NT, preferred_element_type=jnp.float32)
    squares = jnp.sum(rows_f * rows_f, axis=1, keepdims=True)
    row = lax.broadcasted_iota(jnp.int32, (rows_total, 1), 0)
    rest = part // own
    near = row // own % rest < rest // 2
    here = jnp.sum(jnp.where(near, squares, 0.0), axis=0, keepdims=True) / batch_rows
    far = jnp.sum(jnp.where(near, 0.0, squares), axis=0, keepdims=True) / batch_rows
    scales = jnp.sqrt(width / jnp.where(near, here, far))
    scales_ref[...] = scales
    sharp = SHARP * (scales * projected + bias_ref[...])
    latents = jax.nn.softplus(sharp) / SHARP
    sharp_ref[...] = sharp
    latents_ref[...] = latents
    _, there = core_columns(width // 2)
    send_ref[...] = jnp.dot(
        latents.astype(jnp.bfloat16), weight_ref[:, there], preferred_element_type=jnp.float32
    ).astype(jnp.bfloat16)


def encode(parts, weight, enc_bias, own):
    count, width = weight.shape
    rows_total = 4 * parts[0].shape[0]
    f32 = jnp.float32
    return pl.pallas_call(
        functools.partial(encode_kernel, own),
        out_shape=(
            jax.ShapeDtypeStruct((rows_total, width // 2), jnp.bfloat16),
            jax.ShapeDtypeStruct((rows_total, width), jnp.bfloat16),
            jax.ShapeDtypeStruct((rows_total, count), f32),
            jax.ShapeDtypeStruct((rows_total, count), f32),
            jax.ShapeDtypeStruct((rows_total, 1), f32),
        ),
        in_specs=[whole()] * 6,
        out_specs=[whole()] * 5,
        scratch_shapes=[pltpu.VMEM((rows_total, width), f32)],
        compiler_params=pltpu.CompilerParams(vmem_limit_bytes=VMEM_BYTES),
        name="encode",
    )(*parts, weight, enc_bias.reshape(1, count))


def keep_kernel(rides, latents_ref, sharp_ref, weight_ref, *refs):
    half = weight_ref.shape[1] // 2
    latents = latents_ref[...]
    if rides:
        *refs, leaving_ref, staying_ref, packed_ref = refs
    *sources, mine_ref, gate_ref, norms_ref, pull_ref = refs
    here, _ = core_columns(half)
    mine_ref[...] = jnp.dot(
        latents.astype(jnp.bfloat16), weight_ref[:, here], preferred_element_type=jnp.float32
    )
    gate_ref[...] = jax.nn.sigmoid(sharp_ref[...])
    weight_f = weight_ref[...].astype(jnp.float32)
    squares = jnp.sum(weight_f * weight_f, axis=1, keepdims=True)
    squares = jnp.broadcast_to(squares, (squares.shape[0], 128)).T
    norms = jnp.sqrt(squares[:1] + 1e-06)
    norms_ref[...] = norms
    counts = jnp.sum(latents, axis=0, keepdims=True)
    pull = SPARSITY / (latents.shape[0] // 2) * counts / norms
    pull_ref[...] = jnp.broadcast_to(pull, squares.shape).T[:, :1]
    if rides:
        own = staying_ref.shape[1]
        shares = packed_ref.shape[1]
        below = len(sources) * own
        for index, ref in enumerate(sources):
            start = ref.shape[1] - 2 * shares
            value = ref[:, start:].astype(jnp.float32)
            staying_ref[index] = value[:own]
            rows = slice(index * own, (index + 1) * own)
            packed_ref[rows] = value[own:, :shares]
            rows = slice(below + index * own, below + (index + 1) * own)
            packed_ref[rows] = value[own:, shares:]
        leaving_ref[...] = packed_ref[...].astype(jnp.bfloat16)


def keep(latents, sharp, weight, sources, own, shares):
    rows_total, count = latents.shape
    width = weight.shape[1]
    f32 = jnp.float32
    out_shape = [
        jax.ShapeDtypeStruct((rows_total, width // 2), f32),
        jax.ShapeDtypeStruct((rows_total, count), f32),
        jax.ShapeDtypeStruct((1, count), f32),
        jax.ShapeDtypeStruct((count, 1), f32),
    ]
    scratch = []
    if sources:
        out_shape += [
            jax.ShapeDtypeStruct((rows_total, shares), jnp.bfloat16),
            jax.ShapeDtypeStruct((len(sources), own, 2 * shares), f32),
        ]
        scratch = [pltpu.VMEM((rows_total, shares), f32)]
    return pl.pallas_call(
        functools.partial(keep_kernel, bool(sources)),
        out_shape=out_shape,
        in_specs=[whole()] * (3 + len(sources)),
        out_specs=[whole()] * len(out_shape),
        scratch_shapes=scratch,
        compiler_params=pltpu.CompilerParams(vmem_limit_bytes=VMEM_BYTES),
        cost_estimate=pl.CostEstimate(
            flops=rows_total * count * width, bytes_accessed=count * width, transcendentals=0
        ),
        name="keep",
    )(latents, sharp, weight, *sources)


def merge_kernel(distances, total_ref, *refs):
    total = total_ref[...]
    for distance, ref in zip(distances, refs):
        total = total + flip_rows(ref[...].astype(jnp.float32), distance)
    *riders, sum_ref, sent_ref = refs[len(distances) :]
    sum_ref[...] = total
    half = total.shape[1]
    sent_ref[:, :half] = total.astype(jnp.bfloat16)
    for rider in riders:
        sent_ref[:, half:] = rider[...]


def merge(total, arrived, distances, riders=()):
    rows_total, half = total.shape
    wide = half + sum(rider.shape[1] for rider in riders)
    return pl.pallas_call(
        functools.partial(merge_kernel, distances),
        out_shape=(
            jax.ShapeDtypeStruct(total.shape, jnp.float32),
            jax.ShapeDtypeStruct((rows_total, wide), jnp.bfloat16),
        ),
        in_specs=[whole()] * (1 + len(arrived) + len(riders)),
        out_specs=[whole()] * 2,
        compiler_params=pltpu.CompilerParams(vmem_limit_bytes=VMEM_BYTES),
        name="merge",
    )(total, *arrived, *riders)


def settle_kernel(distance, total_ref, arrived_ref, rows_ref, scales_ref, bias_ref, grad_ref):
    rows_total, width = rows_ref.shape
    here, _ = core_columns(width // 2)
    arrived = arrived_ref[:, : width // 2].astype(jnp.float32)
    total = total_ref[...] + flip_rows(arrived, distance)
    target = rows_ref[:, here].astype(jnp.float32) * scales_ref[...]
    error = total + bias_ref[:, here] - target
    grad_ref[...] = (2.0 / (rows_total // 2) * error).astype(jnp.bfloat16)


def settle(total, arrived, rows, scales, dec_bias, distance):
    return pl.pallas_call(
        functools.partial(settle_kernel, distance),
        out_shape=jax.ShapeDtypeStruct(total.shape, jnp.bfloat16),
        in_specs=[whole()] * 5,
        out_specs=whole(),
        compiler_params=pltpu.CompilerParams(vmem_limit_bytes=VMEM_BYTES),
        name="settle",
    )(total, arrived, rows, scales, dec_bias.reshape(1, -1))


def early_kernel(grad_ref, weight_ref, norms_ref, out_ref):
    here, _ = core_columns(weight_ref.shape[1] // 2)
    batch_rows = grad_ref.shape[0] // 2
    out_ref[...] = (
        lax.dot_general(
            grad_ref[...], weight_ref[:, here], NT, preferred_element_type=jnp.float32
        )
        + SPARSITY / batch_rows * norms_ref[...]
    )


def early(grad_mine, weight, norms):
    rows_total, half = grad_mine.shape
    count = weight.shape[0]
    return pl.pallas_call(
        early_kernel,
        out_shape=jax.ShapeDtypeStruct((rows_total, count), jnp.float32),
        in_specs=[whole()] * 3,
        out_specs=whole(),
        compiler_params=pltpu.CompilerParams(vmem_limit_bytes=VMEM_BYTES),
        cost_estimate=pl.CostEstimate(
            flops=2 * rows_total * count * half, bytes_accessed=count * half, transcendentals=0
        ),
        name="early",
    )(grad_mine, weight, norms)


def finish_kernel(
    tile,
    span,
    rides,
    grad_ref,
    early_ref,
    rows_ref,
    weight_ref,
    latents_ref,
    gate_ref,
    scales_ref,
    pull_ref,
    *refs,
):
    if rides:
        arrived_ref, staying_ref, weight_grad_hbm, bias_grad_hbm, dec_grad_hbm, next_hbm = refs[:6]
        staged_ref, bias_ref, dec_ref, sums_ref, left_ref, sems, blocks_ref, line_ref, next_ref = (
            refs[6:]
        )
    else:
        weight_grad_hbm, bias_grad_hbm, dec_grad_hbm = refs[:3]
        staged_ref, bias_ref, dec_ref, sums_ref, left_ref, sems = refs[3:]
    rows_total, width = rows_ref.shape
    shares = dec_grad_hbm.shape[0]
    count = width // tile
    core = lax.axis_index("latent")
    _, there = core_columns(width // 2)
    grad_latents = early_ref[...] + lax.dot_general(
        grad_ref[:, there], weight_ref[:, there], NT, preferred_element_type=jnp.float32
    )
    grad_pre = grad_latents * gate_ref[...]
    bias_ref[...] = jnp.sum(grad_pre, axis=0, keepdims=True)
    bias_copy = pltpu.make_async_copy(bias_ref, bias_grad_hbm, sems.at[count])
    bias_copy.start()
    left = jnp.concatenate([grad_pre * scales_ref[...], latents_ref[...]], axis=0)
    left_ref[...] = left.T.astype(jnp.bfloat16)

    sums = jnp.sum(grad_ref[...].astype(jnp.float32), axis=0, keepdims=True)
    sums_ref[:, :width] = jnp.broadcast_to(sums, (8, width))
    sums_ref[:, width:] = jnp.zeros((8, span), jnp.float32)
    offset = lax.axis_index(("dp", "latent")) * shares
    lead = lax.rem(offset, 128)
    window = sums_ref[:, pl.ds(pl.multiple_of(offset - lead, 128), span)]
    window = pltpu.roll(window, lax.rem(span - lead, span), 1)
    dec_ref[...] = window[0, :shares]
    dec_copy = pltpu.make_async_copy(dec_ref, dec_grad_hbm, sems.at[count + 1])
    dec_copy.start()

    if rides:
        near, own, columns = staying_ref.shape
        came = arrived_ref[:, width // 2 :].astype(jnp.float32)
        for index in range(near):
            blocks_ref[index] = staying_ref[index]
            rows = slice(index * own, (index + 1) * own)
            blocks_ref[near + index, :, :shares] = came[rows]
            rows = slice((near + index) * own, (near + index + 1) * own)
            blocks_ref[near + index, :, shares:] = came[rows]
        place = lax.axis_index("dp")
        for source in range(2 * near):
            line_ref[:, source * columns : (source + 1) * columns] = blocks_ref[place ^ source]
        next_ref[...] = line_ref[...].astype(jnp.bfloat16)
        next_copy = pltpu.make_async_copy(next_ref, next_hbm, sems.at[count + 2])
        next_copy.start()

    copies = [
        pltpu.make_async_copy(
            staged_ref.at[:, pl.ds(index * tile, tile)],
            weight_grad_hbm.at[:, pl.ds(index * tile, tile)],
            sems.at[index],
        )
        for index in range(count)
    ]

    @pl.loop(0, 1 + core // 2)
    def _(_):
        pull = pull_ref[...]
        for index in range(count):
            columns = slice(index * tile, (index + 1) * tile)
            right = jnp.concatenate([rows_ref[:, columns], grad_ref[:, columns]], axis=0)
            total = jnp.dot(left_ref[...], right, preferred_element_type=jnp.float32)
            total = total + pull * weight_ref[:, columns].astype(jnp.float32)
            staged_ref[:, columns] = total.astype(jnp.bfloat16)
            copies[index].start()

    for copy in copies:
        copy.wait()
    bias_copy.wait()
    dec_copy.wait()
    if rides:
        next_copy.wait()


def finish(grad_out, early_sum, rows, weight, latents, gate, scales, pull, shares, riders):
    rows_total, width = rows.shape
    count = weight.shape[0]
    tile = 768
    span = (shares + 127 + 127) // 128 * 128
    f32 = jnp.float32
    out_shape = [
        jax.ShapeDtypeStruct((count, width), jnp.bfloat16),
        jax.ShapeDtypeStruct((1, count), f32),
        jax.ShapeDtypeStruct((shares,), f32),
    ]
    scratch = [
        pltpu.VMEM((count, width), jnp.bfloat16),
        pltpu.VMEM((1, count), f32),
        pltpu.VMEM((shares,), f32),
        pltpu.VMEM((8, width + span), f32),
        pltpu.VMEM((count, 2 * rows_total), jnp.bfloat16),
        pltpu.SemaphoreType.DMA((width // tile + 3,)),
    ]
    if riders:
        near, own, columns = riders[1].shape
        out_shape.append(jax.ShapeDtypeStruct((own, width), jnp.bfloat16))
        scratch += [
            pltpu.VMEM((2 * near, own, columns), f32),
            pltpu.VMEM((own, width), f32),
            pltpu.VMEM((own, width), jnp.bfloat16),
        ]
    return pl.pallas_call(
        functools.partial(finish_kernel, tile, span, bool(riders)),
        out_shape=out_shape,
        in_specs=[whole()] * (8 + len(riders)),
        out_specs=[whole(pl.ANY)] * len(out_shape),
        scratch_shapes=scratch,
        compiler_params=pltpu.CompilerParams(vmem_limit_bytes=VMEM_BYTES),
        name="finish",
    )(grad_out, early_sum, rows, weight, latents, gate, scales, pull, *riders)


def shuffle_rest(riders, dp, own, columns):
    place = lax.axis_index("dp")
    distance = 4
    while distance < dp:
        split = riders.reshape((-1, 2) + riders.shape[1:])
        riders = jnp.concatenate([split[:, 0], exchange(split[:, 1], "dp", distance)], axis=1)
        distance *= 2
    riders = riders[0]
    bit = 1
    while bit < dp:
        pairs = riders.reshape(dp // (2 * bit), 2, bit * own * columns)
        pairs = jnp.where(place & bit == 0, pairs, pairs[:, ::-1])
        riders = pairs.reshape(dp, own, columns)
        bit *= 2
    return riders.transpose(1, 0, 2).reshape(own, dp * columns)


def per_device(cur_rows, cached_rows, shuffle_perm, weight, enc_bias, dec_bias):
    dp = lax.axis_size("dp")
    rest = dp // 4
    own, width = cur_rows.shape
    columns = cached_rows.shape[1]
    count = weight.shape[0]
    shares = width // (2 * dp)
    core = lax.axis_index("latent")

    came = exchange(cur_rows, "dp", 4)
    ordered, cur_copy, weight = order(cur_rows, cached_rows, shuffle_perm, weight)
    near = jnp.concatenate([cur_copy, came], axis=0)
    distance = 8
    while distance < dp:
        near = jnp.concatenate([near, exchange(near, "dp", distance)], axis=0)
        distance *= 2
    ordered = ordered.reshape(4, rest * own, columns)
    parts = [near] + [
        exchange(jnp.concatenate([near, ordered[low]], axis=1), "dp", low) for low in range(1, 4)
    ]

    send, gathered, latents, sharp, scales = encode(parts, weight, enc_bias, own)
    came = exchange(send, "latent", 1)
    rides = rest == 2
    sources = [ordered[0]] + parts[1:] if rides else []
    mine, gate, norms, pull, *riders = keep(latents, sharp, weight, sources, own, shares)

    total = mine + came.astype(jnp.float32)
    sent = total.astype(jnp.bfloat16)
    lows = (1, 2, 3)
    total, sent = merge(
        total,
        [exchange(sent, "dp", low) for low in lows],
        tuple(low * rest * own for low in lows),
        riders[:1],
    )
    distance = 4
    while distance < dp:
        arrived = exchange(sent, "dp", distance)
        row_distance = distance // 4 * own
        if 2 * distance < dp:
            total, sent = merge(total, [arrived], (row_distance,))
        else:
            grad_mine = settle(total, arrived, gathered, scales, dec_bias, row_distance)
        distance *= 2

    grad_other = exchange(grad_mine, "latent", 1)
    early_sum = early(grad_mine, weight, norms)
    low_half = jnp.where(core == 0, grad_mine, grad_other)
    high_half = jnp.where(core == 0, grad_other, grad_mine)
    grad_out = jnp.concatenate([low_half, high_half], axis=1)
    weight_grad, enc_bias_grad, dec_bias_grad, *shuffled = finish(
        grad_out,
        early_sum,
        gathered,
        weight,
        latents,
        gate,
        scales,
        pull,
        shares,
        (arrived, riders[1]) if rides else (),
    )
    if rides:
        next_batch = shuffled[0]
    else:
        riders = jnp.stack([ordered[0]] + [part[:, width:] for part in parts[1:]])
        riders = riders.reshape(4, rest, own, columns).transpose(1, 0, 2, 3)
        next_batch = shuffle_rest(riders, dp, own, columns)
    return (weight_grad, enc_bias_grad.reshape(count), dec_bias_grad, next_batch)


def solution(mesh):
    return jax.shard_map(
        per_device,
        mesh=mesh,
        in_specs=(
            P(("group", "dp"), None),
            P("group", "dp"),
            P("group"),
            P(("group", "dp", "latent"), None),
            P(("group", "dp", "latent")),
            P("group"),
        ),
        out_specs=(
            P(("group", "dp", "latent"), None),
            P(("group", "dp", "latent")),
            P(("group", "dp", "latent")),
            P(("group", "dp"), None),
        ),
        check_vma=False,
    )
```

```python
import functools

import jax
import jax.numpy as jnp
from jax import lax
from jax.experimental import pallas as pl
from jax.experimental.pallas import tpu as pltpu
from jax.sharding import PartitionSpec as P

SPARSITY = 4.0
SHARP = 4.0
VMEM_BYTES = 16 * 1024 * 1024
NT = (((1,), (1,)), ((), ()))
TN = (((0,), (0,)), ((), ()))


def whole(space=pltpu.VMEM):
    return pl.BlockSpec(memory_space=space)


def exchange(value, axis, distance):
    size = lax.axis_size(axis)
    return lax.ppermute(value, axis, [(k, k ^ distance) for k in range(size)])


def core_columns(half):
    core = lax.axis_index("latent")
    here = pl.ds(pl.multiple_of(core * half, 128), half)
    there = pl.ds(pl.multiple_of((1 - core) * half, 128), half)
    return here, there


def flip_rows(value, distance):
    count = value.shape[0]
    row = lax.broadcasted_iota(jnp.int32, value.shape, 0)
    bit = 1
    while bit <= distance:
        if distance & bit:
            up = pltpu.roll(value, count - bit, 0)
            down = pltpu.roll(value, bit, 0)
            value = jnp.where(row & bit == 0, up, down)
        bit *= 2
    return value


def order_kernel(
    turn,
    cur_hbm,
    cached_hbm,
    perm_hbm,
    weight_hbm,
    out_ref,
    cur_ref,
    weight_ref,
    cached_ref,
    perm_ref,
    sems,
):
    row_total, columns = cached_ref.shape
    own = cur_ref.shape[0]
    dp = row_total // own
    fetches = [
        pltpu.make_async_copy(cached_hbm, cached_ref, sems.at[0]),
        pltpu.make_async_copy(perm_hbm, perm_ref, sems.at[1]),
        pltpu.make_async_copy(cur_hbm, cur_ref, sems.at[2]),
        pltpu.make_async_copy(weight_hbm, weight_ref, sems.at[3]),
    ]
    for fetch in fetches:
        fetch.start()
    row = lax.broadcasted_iota(jnp.int32, (row_total, row_total), 0)
    rest = dp // 4
    low, high = row // (rest * own), row // own % rest
    distance = (low ^ (turn * high)) + 4 * high
    wanted = (distance ^ lax.axis_index("dp")) * own + row % own
    for fetch in fetches[:2]:
        fetch.wait()
    selector = (jnp.broadcast_to(perm_ref[...], row.shape) == wanted).astype(jnp.bfloat16)
    out_ref[...] = jnp.dot(
        selector, cached_ref[...], preferred_element_type=jnp.float32
    ).astype(jnp.bfloat16)
    for fetch in fetches[2:]:
        fetch.wait()


def order(cur_rows, cached_rows, shuffle_perm, weight, turn):
    row_total, columns = cached_rows.shape
    return pl.pallas_call(
        functools.partial(order_kernel, turn),
        out_shape=(
            jax.ShapeDtypeStruct((row_total, columns), jnp.bfloat16),
            jax.ShapeDtypeStruct(cur_rows.shape, jnp.bfloat16),
            jax.ShapeDtypeStruct(weight.shape, jnp.bfloat16),
        ),
        in_specs=[whole(pl.ANY)] * 4,
        out_specs=[whole()] * 3,
        scratch_shapes=[
            pltpu.VMEM((row_total, columns), jnp.bfloat16),
            pltpu.VMEM((1, row_total), jnp.int32),
            pltpu.SemaphoreType.DMA((4,)),
        ],
        compiler_params=pltpu.CompilerParams(vmem_limit_bytes=VMEM_BYTES),
        cost_estimate=pl.CostEstimate(flops=4000000, bytes_accessed=2000000, transcendentals=0),
        name="order",
    )(
        *(
            pltpu.with_memory_space_constraint(value, pltpu.MemorySpace.HBM)
            for value in (cur_rows, cached_rows, shuffle_perm.reshape(1, row_total), weight)
        )
    )


def encode_kernel(
    own,
    first_ref,
    second_ref,
    third_ref,
    fourth_ref,
    weight_ref,
    bias_ref,
    send_ref,
    rows_ref,
    latents_ref,
    sharp_ref,
    scales_ref,
    rows_f_ref,
    scaled_ref,
):
    rows_total, width = rows_f_ref.shape
    batch_rows = rows_total // 2
    part = rows_total // 4
    for index, ref in enumerate((first_ref, second_ref, third_ref, fourth_ref)):
        value = ref[...].astype(jnp.float32)
        rows_f_ref[index * part : (index + 1) * part] = value[:, :width]
    rows_f = rows_f_ref[...]
    rows = rows_f.astype(jnp.bfloat16)
    rows_ref[...] = rows
    projected = lax.dot_general(rows, weight_ref[...], NT, preferred_element_type=jnp.float32)
    squares = jnp.sum(rows_f * rows_f, axis=1, keepdims=True)
    row = lax.broadcasted_iota(jnp.int32, (rows_total, 1), 0)
    rest = part // own
    near = row // own % rest < rest // 2
    here = jnp.sum(jnp.where(near, squares, 0.0), axis=0, keepdims=True) / batch_rows
    far = jnp.sum(jnp.where(near, 0.0, squares), axis=0, keepdims=True) / batch_rows
    scales = jnp.sqrt(width / jnp.where(near, here, far))
    scales_ref[...] = scales
    scaled_ref[...] = scales * projected

    @pl.loop(0, 1 + lax.axis_index("latent") // 2)
    def _(_):
        sharp = SHARP * (scaled_ref[...] + bias_ref[...])
        latents = jax.nn.softplus(sharp) / SHARP
        sharp_ref[...] = sharp
        latents_ref[...] = latents
        _, there = core_columns(width // 2)
        send_ref[...] = jnp.dot(
            latents.astype(jnp.bfloat16),
            weight_ref[:, there],
            preferred_element_type=jnp.float32,
        ).astype(jnp.bfloat16)


def encode(parts, weight, enc_bias, own):
    count, width = weight.shape
    rows_total = 4 * parts[0].shape[0]
    f32 = jnp.float32
    return pl.pallas_call(
        functools.partial(encode_kernel, own),
        out_shape=(
            jax.ShapeDtypeStruct((rows_total, width // 2), jnp.bfloat16),
            jax.ShapeDtypeStruct((rows_total, width), jnp.bfloat16),
            jax.ShapeDtypeStruct((rows_total, count), f32),
            jax.ShapeDtypeStruct((rows_total, count), f32),
            jax.ShapeDtypeStruct((rows_total, 1), f32),
        ),
        in_specs=[whole()] * 6,
        out_specs=[whole()] * 5,
        scratch_shapes=[pltpu.VMEM((rows_total, width), f32), pltpu.VMEM((rows_total, count), f32)],
        compiler_params=pltpu.CompilerParams(vmem_limit_bytes=VMEM_BYTES),
        name="encode",
    )(*parts, weight, enc_bias.reshape(1, count))


def keep_kernel(rides, latents_ref, sharp_ref, weight_ref, *refs):
    half = weight_ref.shape[1] // 2
    latents = latents_ref[...]
    if rides:
        *refs, leaving_ref, staying_ref, packed_ref = refs
    *sources, mine_ref, gate_ref, norms_ref, pull_ref = refs
    here, _ = core_columns(half)
    mine_ref[...] = jnp.dot(
        latents.astype(jnp.bfloat16), weight_ref[:, here], preferred_element_type=jnp.float32
    )
    gate_ref[...] = jax.nn.sigmoid(sharp_ref[...])
    weight_f = weight_ref[...].astype(jnp.float32)
    squares = jnp.sum(weight_f * weight_f, axis=1, keepdims=True)
    squares = jnp.broadcast_to(squares, (squares.shape[0], 128)).T
    norms = jnp.sqrt(squares[:1] + 1e-06)
    norms_ref[...] = norms
    counts = jnp.sum(latents, axis=0, keepdims=True)
    pull = SPARSITY / (latents.shape[0] // 2) * counts / norms
    pull_ref[...] = jnp.broadcast_to(pull, squares.shape).T[:, :1]
    if rides:
        own = staying_ref.shape[1]
        shares = packed_ref.shape[1]
        below = len(sources) * own
        for index, ref in enumerate(sources):
            start = ref.shape[1] - 2 * shares
            value = ref[:, start:].astype(jnp.float32)
            staying_ref[index] = value[:own]
            rows = slice(index * own, (index + 1) * own)
            packed_ref[rows] = value[own:, :shares]
            rows = slice(below + index * own, below + (index + 1) * own)
            packed_ref[rows] = value[own:, shares:]
        leaving_ref[...] = packed_ref[...].astype(jnp.bfloat16)


def keep(latents, sharp, weight, sources, own, shares):
    rows_total, count = latents.shape
    width = weight.shape[1]
    f32 = jnp.float32
    out_shape = [
        jax.ShapeDtypeStruct((rows_total, width // 2), f32),
        jax.ShapeDtypeStruct((rows_total, count), f32),
        jax.ShapeDtypeStruct((1, count), f32),
        jax.ShapeDtypeStruct((count, 1), f32),
    ]
    scratch = []
    if sources:
        out_shape += [
            jax.ShapeDtypeStruct((rows_total, shares), jnp.bfloat16),
            jax.ShapeDtypeStruct((len(sources), own, 2 * shares), f32),
        ]
        scratch = [pltpu.VMEM((rows_total, shares), f32)]
    return pl.pallas_call(
        functools.partial(keep_kernel, bool(sources)),
        out_shape=out_shape,
        in_specs=[whole()] * (3 + len(sources)),
        out_specs=[whole()] * len(out_shape),
        scratch_shapes=scratch,
        compiler_params=pltpu.CompilerParams(vmem_limit_bytes=VMEM_BYTES),
        cost_estimate=pl.CostEstimate(
            flops=rows_total * count * width, bytes_accessed=count * width, transcendentals=0
        ),
        name="keep",
    )(latents, sharp, weight, *sources)


def merge_kernel(distances, total_ref, *refs):
    total = total_ref[...]
    for distance, ref in zip(distances, refs):
        total = total + flip_rows(ref[...].astype(jnp.float32), distance)
    *riders, sum_ref, sent_ref = refs[len(distances) :]
    sum_ref[...] = total
    half = total.shape[1]
    sent_ref[:, :half] = total.astype(jnp.bfloat16)
    for rider in riders:
        sent_ref[:, half:] = rider[...]


def merge(total, arrived, distances, riders=()):
    rows_total, half = total.shape
    wide = half + sum(rider.shape[1] for rider in riders)
    return pl.pallas_call(
        functools.partial(merge_kernel, distances),
        out_shape=(
            jax.ShapeDtypeStruct(total.shape, jnp.float32),
            jax.ShapeDtypeStruct((rows_total, wide), jnp.bfloat16),
        ),
        in_specs=[whole()] * (1 + len(arrived) + len(riders)),
        out_specs=[whole()] * 2,
        compiler_params=pltpu.CompilerParams(vmem_limit_bytes=VMEM_BYTES),
        name="merge",
    )(total, *arrived, *riders)


def settle_kernel(distance, total_ref, arrived_ref, rows_ref, scales_ref, bias_ref, grad_ref):
    rows_total, width = rows_ref.shape
    here, _ = core_columns(width // 2)
    arrived = arrived_ref[:, : width // 2].astype(jnp.float32)
    total = total_ref[...] + flip_rows(arrived, distance)
    target = rows_ref[:, here].astype(jnp.float32) * scales_ref[...]
    error = total + bias_ref[:, here] - target
    grad_ref[...] = (2.0 / (rows_total // 2) * error).astype(jnp.bfloat16)


def settle(total, arrived, rows, scales, dec_bias, distance):
    return pl.pallas_call(
        functools.partial(settle_kernel, distance),
        out_shape=jax.ShapeDtypeStruct(total.shape, jnp.bfloat16),
        in_specs=[whole()] * 5,
        out_specs=whole(),
        compiler_params=pltpu.CompilerParams(vmem_limit_bytes=VMEM_BYTES),
        name="settle",
    )(total, arrived, rows, scales, dec_bias.reshape(1, -1))


def early_kernel(grad_ref, weight_ref, norms_ref, out_ref):
    here, _ = core_columns(weight_ref.shape[1] // 2)
    batch_rows = grad_ref.shape[0] // 2
    out_ref[...] = (
        lax.dot_general(
            grad_ref[...], weight_ref[:, here], NT, preferred_element_type=jnp.float32
        )
        + SPARSITY / batch_rows * norms_ref[...]
    )


def early(grad_mine, weight, norms):
    rows_total, half = grad_mine.shape
    count = weight.shape[0]
    return pl.pallas_call(
        early_kernel,
        out_shape=jax.ShapeDtypeStruct((rows_total, count), jnp.float32),
        in_specs=[whole()] * 3,
        out_specs=whole(),
        compiler_params=pltpu.CompilerParams(vmem_limit_bytes=VMEM_BYTES),
        cost_estimate=pl.CostEstimate(
            flops=2 * rows_total * count * half, bytes_accessed=count * half, transcendentals=0
        ),
        name="early",
    )(grad_mine, weight, norms)


def finish_kernel(
    tile,
    span,
    rides,
    turn,
    mine_ref,
    other_ref,
    early_ref,
    rows_ref,
    weight_ref,
    latents_ref,
    gate_ref,
    scales_ref,
    pull_ref,
    *refs,
):
    if rides:
        arrived_ref, staying_ref, weight_grad_hbm, bias_grad_hbm, dec_grad_hbm, next_hbm = refs[:6]
        *refs, blocks_ref, line_ref, next_ref = refs[6:]
    else:
        weight_grad_hbm, bias_grad_hbm, dec_grad_hbm, *refs = refs
    grad_ref, staged_ref, bias_ref, dec_ref, sums_ref, left_ref, sems = refs
    rows_total, width = rows_ref.shape
    shares = dec_grad_hbm.shape[0]
    count = width // tile
    core = lax.axis_index("latent")
    here, there = core_columns(width // 2)
    grad_latents = early_ref[...] + lax.dot_general(
        other_ref[...], weight_ref[:, there], NT, preferred_element_type=jnp.float32
    )
    grad_ref[:, here] = mine_ref[...]
    grad_ref[:, there] = other_ref[...]
    grad_pre = grad_latents * gate_ref[...]
    bias_ref[...] = jnp.sum(grad_pre, axis=0, keepdims=True)
    bias_copy = pltpu.make_async_copy(bias_ref, bias_grad_hbm, sems.at[count])
    bias_copy.start()
    left = jnp.concatenate([grad_pre * scales_ref[...], latents_ref[...]], axis=0)
    left_ref[...] = left.T.astype(jnp.bfloat16)

    sums = jnp.sum(grad_ref[...].astype(jnp.float32), axis=0, keepdims=True)
    sums_ref[:, :width] = jnp.broadcast_to(sums, (8, width))
    sums_ref[:, width:] = jnp.zeros((8, span), jnp.float32)
    offset = lax.axis_index(("dp", "latent")) * shares
    lead = lax.rem(offset, 128)
    window = sums_ref[:, pl.ds(pl.multiple_of(offset - lead, 128), span)]
    window = pltpu.roll(window, lax.rem(span - lead, span), 1)
    dec_ref[...] = window[0, :shares]
    dec_copy = pltpu.make_async_copy(dec_ref, dec_grad_hbm, sems.at[count + 1])
    dec_copy.start()

    if rides:
        near, own, columns = staying_ref.shape
        came = arrived_ref[:, width // 2 :].astype(jnp.float32)
        for index in range(near):
            blocks_ref[index] = staying_ref[index]
            rows = slice(index * own, (index + 1) * own)
            blocks_ref[near + index, :, :shares] = came[rows]
            rows = slice((near + index) * own, (near + index + 1) * own)
            blocks_ref[near + index, :, shares:] = came[rows]
        place = lax.axis_index("dp")
        for source in range(2 * near):
            away = place ^ source
            away = away ^ (turn * (away // near))
            line_ref[:, source * columns : (source + 1) * columns] = blocks_ref[away]
        next_ref[...] = line_ref[...].astype(jnp.bfloat16)
        next_copy = pltpu.make_async_copy(next_ref, next_hbm, sems.at[count + 2])
        next_copy.start()

    copies = [
        pltpu.make_async_copy(
            staged_ref.at[:, pl.ds(index * tile, tile)],
            weight_grad_hbm.at[:, pl.ds(index * tile, tile)],
            sems.at[index],
        )
        for index in range(count)
    ]

    @pl.loop(0, 1 + core // 2)
    def _(_):
        pull = pull_ref[...]
        for index in range(count):
            columns = slice(index * tile, (index + 1) * tile)
            right = jnp.concatenate([rows_ref[:, columns], grad_ref[:, columns]], axis=0)
            total = jnp.dot(left_ref[...], right, preferred_element_type=jnp.float32)
            total = total + pull * weight_ref[:, columns].astype(jnp.float32)
            staged_ref[:, columns] = total.astype(jnp.bfloat16)
            copies[index].start()

    for copy in copies:
        copy.wait()
    bias_copy.wait()
    dec_copy.wait()
    if rides:
        next_copy.wait()


def finish(mine, other, early_sum, rows, weight, latents, gate, scales, pull, shares, riders, turn):
    rows_total, width = rows.shape
    count = weight.shape[0]
    tile = 768
    span = (shares + 127 + 127) // 128 * 128
    f32 = jnp.float32
    out_shape = [
        jax.ShapeDtypeStruct((count, width), jnp.bfloat16),
        jax.ShapeDtypeStruct((1, count), f32),
        jax.ShapeDtypeStruct((shares,), f32),
    ]
    scratch = [
        pltpu.VMEM((rows_total, width), jnp.bfloat16),
        pltpu.VMEM((count, width), jnp.bfloat16),
        pltpu.VMEM((1, count), f32),
        pltpu.VMEM((shares,), f32),
        pltpu.VMEM((8, width + span), f32),
        pltpu.VMEM((count, 2 * rows_total), jnp.bfloat16),
        pltpu.SemaphoreType.DMA((width // tile + 3,)),
    ]
    if riders:
        near, own, columns = riders[1].shape
        out_shape.append(jax.ShapeDtypeStruct((own, width), jnp.bfloat16))
        scratch += [
            pltpu.VMEM((2 * near, own, columns), f32),
            pltpu.VMEM((own, width), f32),
            pltpu.VMEM((own, width), jnp.bfloat16),
        ]
    return pl.pallas_call(
        functools.partial(finish_kernel, tile, span, bool(riders), turn),
        out_shape=out_shape,
        in_specs=[whole()] * (9 + len(riders)),
        out_specs=[whole(pl.ANY)] * len(out_shape),
        scratch_shapes=scratch,
        compiler_params=pltpu.CompilerParams(vmem_limit_bytes=VMEM_BYTES),
        name="finish",
    )(mine, other, early_sum, rows, weight, latents, gate, scales, pull, *riders)


def shuffle_rest(riders, dp, own, columns):
    place = lax.axis_index("dp")
    distance = 4
    while distance < dp:
        split = riders.reshape((-1, 2) + riders.shape[1:])
        riders = jnp.concatenate([split[:, 0], exchange(split[:, 1], "dp", distance)], axis=1)
        distance *= 2
    riders = riders[0]
    bit = 1
    while bit < dp:
        pairs = riders.reshape(dp // (2 * bit), 2, bit * own * columns)
        pairs = jnp.where(place & bit == 0, pairs, pairs[:, ::-1])
        riders = pairs.reshape(dp, own, columns)
        bit *= 2
    return riders.transpose(1, 0, 2).reshape(own, dp * columns)


def per_device(cur_rows, cached_rows, shuffle_perm, weight, enc_bias, dec_bias):
    dp = lax.axis_size("dp")
    rest = dp // 4
    own, width = cur_rows.shape
    columns = cached_rows.shape[1]
    count = weight.shape[0]
    shares = width // (2 * dp)

    rides = rest == 2
    turn = 2 if rides else 0

    came = exchange(cur_rows, "dp", 4)
    ordered, cur_copy, weight = order(cur_rows, cached_rows, shuffle_perm, weight, turn)
    near = jnp.concatenate([cur_copy, came], axis=0)
    distance = 8
    while distance < dp:
        near = jnp.concatenate([near, exchange(near, "dp", distance)], axis=0)
        distance *= 2
    ordered = ordered.reshape(4, rest * own, columns)
    parts = [near] + [
        exchange(jnp.concatenate([near, ordered[low]], axis=1), "dp", low) for low in range(1, 4)
    ]

    send, gathered, latents, sharp, scales = encode(parts, weight, enc_bias, own)
    came = exchange(send, "latent", 1)
    sources = [ordered[0]] + parts[1:] if rides else []
    mine, gate, norms, pull, *riders = keep(latents, sharp, weight, sources, own, shares)

    total = mine + came.astype(jnp.float32)
    sent = total.astype(jnp.bfloat16)
    lows = (1, 2, 3)
    total, sent = merge(
        total,
        [exchange(sent, "dp", low) for low in lows],
        tuple(low * rest * own for low in lows),
        riders[:1],
    )
    distance = 4
    while distance < dp:
        arrived = exchange(sent, "dp", distance + turn)
        row_distance = distance // 4 * own + turn * rest * own
        if 2 * distance < dp:
            total, sent = merge(total, [arrived], (row_distance,))
        else:
            grad_mine = settle(total, arrived, gathered, scales, dec_bias, row_distance)
        distance *= 2

    grad_other = exchange(grad_mine, "latent", 1)
    early_sum = early(grad_mine, weight, norms)
    weight_grad, enc_bias_grad, dec_bias_grad, *shuffled = finish(
        grad_mine,
        grad_other,
        early_sum,
        gathered,
        weight,
        latents,
        gate,
        scales,
        pull,
        shares,
        (arrived, riders[1]) if rides else (),
        turn,
    )
    if rides:
        next_batch = shuffled[0]
    else:
        riders = jnp.stack([ordered[0]] + [part[:, width:] for part in parts[1:]])
        riders = riders.reshape(4, rest, own, columns).transpose(1, 0, 2, 3)
        next_batch = shuffle_rest(riders, dp, own, columns)
    return (weight_grad, enc_bias_grad.reshape(count), dec_bias_grad, next_batch)


def solution(mesh):
    return jax.shard_map(
        per_device,
        mesh=mesh,
        in_specs=(
            P(("group", "dp"), None),
            P("group", "dp"),
            P("group"),
            P(("group", "dp", "latent"), None),
            P(("group", "dp", "latent")),
            P("group"),
        ),
        out_specs=(
            P(("group", "dp", "latent"), None),
            P(("group", "dp", "latent")),
            P(("group", "dp", "latent")),
            P(("group", "dp"), None),
        ),
        check_vma=False,
    )
```

```python
import functools

import jax
import jax.numpy as jnp
from jax import lax
from jax.experimental import pallas as pl
from jax.experimental.pallas import tpu as pltpu
from jax.sharding import PartitionSpec as P

SPARSITY = 4.0
SHARP = 4.0
VMEM_BYTES = 16 * 1024 * 1024
NT = (((1,), (1,)), ((), ()))
TN = (((0,), (0,)), ((), ()))


def whole(space=pltpu.VMEM):
    return pl.BlockSpec(memory_space=space)


def exchange(value, axis, distance):
    size = lax.axis_size(axis)
    return lax.ppermute(value, axis, [(k, k ^ distance) for k in range(size)])


def core_columns(half):
    core = lax.axis_index("latent")
    here = pl.ds(pl.multiple_of(core * half, 128), half)
    there = pl.ds(pl.multiple_of((1 - core) * half, 128), half)
    return here, there


def flip_rows(value, distance):
    count = value.shape[0]
    row = lax.broadcasted_iota(jnp.int32, value.shape, 0)
    bit = 1
    while bit <= distance:
        if distance & bit:
            up = pltpu.roll(value, count - bit, 0)
            down = pltpu.roll(value, bit, 0)
            value = jnp.where(row & bit == 0, up, down)
        bit *= 2
    return value


def order_kernel(
    turn,
    cur_hbm,
    cached_hbm,
    perm_hbm,
    weight_hbm,
    out_ref,
    cur_ref,
    weight_ref,
    cached_ref,
    perm_ref,
    sems,
):
    row_total, columns = cached_ref.shape
    own = cur_ref.shape[0]
    dp = row_total // own
    fetches = [
        pltpu.make_async_copy(cached_hbm, cached_ref, sems.at[0]),
        pltpu.make_async_copy(perm_hbm, perm_ref, sems.at[1]),
        pltpu.make_async_copy(cur_hbm, cur_ref, sems.at[2]),
        pltpu.make_async_copy(weight_hbm, weight_ref, sems.at[3]),
    ]
    for fetch in fetches:
        fetch.start()
    row = lax.broadcasted_iota(jnp.int32, (row_total, row_total), 0)
    rest = dp // 4
    low, high = row // (rest * own), row // own % rest
    distance = (low ^ (turn * high)) + 4 * high
    wanted = (distance ^ lax.axis_index("dp")) * own + row % own
    for fetch in fetches[:2]:
        fetch.wait()
    selector = (jnp.broadcast_to(perm_ref[...], row.shape) == wanted).astype(jnp.bfloat16)
    out_ref[...] = jnp.dot(
        selector, cached_ref[...], preferred_element_type=jnp.float32
    ).astype(jnp.bfloat16)
    for fetch in fetches[2:]:
        fetch.wait()


def order(cur_rows, cached_rows, shuffle_perm, weight, turn):
    row_total, columns = cached_rows.shape
    return pl.pallas_call(
        functools.partial(order_kernel, turn),
        out_shape=(
            jax.ShapeDtypeStruct((row_total, columns), jnp.bfloat16),
            jax.ShapeDtypeStruct(cur_rows.shape, jnp.bfloat16),
            jax.ShapeDtypeStruct(weight.shape, jnp.bfloat16),
        ),
        in_specs=[whole(pl.ANY)] * 4,
        out_specs=[whole()] * 3,
        scratch_shapes=[
            pltpu.VMEM((row_total, columns), jnp.bfloat16),
            pltpu.VMEM((1, row_total), jnp.int32),
            pltpu.SemaphoreType.DMA((4,)),
        ],
        compiler_params=pltpu.CompilerParams(vmem_limit_bytes=VMEM_BYTES),
        cost_estimate=pl.CostEstimate(flops=4000000, bytes_accessed=2000000, transcendentals=0),
        name="order",
    )(
        *(
            pltpu.with_memory_space_constraint(value, pltpu.MemorySpace.HBM)
            for value in (cur_rows, cached_rows, shuffle_perm.reshape(1, row_total), weight)
        )
    )


def encode_kernel(
    own,
    first_ref,
    second_ref,
    third_ref,
    fourth_ref,
    weight_ref,
    bias_ref,
    send_ref,
    rows_ref,
    latents_ref,
    sharp_ref,
    scales_ref,
    rows_f_ref,
    scaled_ref,
):
    rows_total, width = rows_f_ref.shape
    batch_rows = rows_total // 2
    part = rows_total // 4
    for index, ref in enumerate((first_ref, second_ref, third_ref, fourth_ref)):
        value = ref[...].astype(jnp.float32)
        rows_f_ref[index * part : (index + 1) * part] = value[:, :width]
    rows_f = rows_f_ref[...]
    rows = rows_f.astype(jnp.bfloat16)
    rows_ref[...] = rows
    projected = lax.dot_general(rows, weight_ref[...], NT, preferred_element_type=jnp.float32)
    squares = jnp.sum(rows_f * rows_f, axis=1, keepdims=True)
    row = lax.broadcasted_iota(jnp.int32, (rows_total, 1), 0)
    rest = part // own
    near = row // own % rest < rest // 2
    here = jnp.sum(jnp.where(near, squares, 0.0), axis=0, keepdims=True) / batch_rows
    far = jnp.sum(jnp.where(near, 0.0, squares), axis=0, keepdims=True) / batch_rows
    scales = jnp.sqrt(width / jnp.where(near, here, far))
    scales_ref[...] = scales
    scaled_ref[...] = scales * projected

    @pl.loop(0, 1 + lax.axis_index("latent") // 2)
    def _(_):
        sharp = SHARP * (scaled_ref[...] + bias_ref[...])
        latents = jax.nn.softplus(sharp) / SHARP
        sharp_ref[...] = sharp
        latents_ref[...] = latents
        _, there = core_columns(width // 2)
        send_ref[...] = jnp.dot(
            latents.astype(jnp.bfloat16),
            weight_ref[:, there],
            preferred_element_type=jnp.float32,
        ).astype(jnp.bfloat16)


def encode(parts, weight, enc_bias, own):
    count, width = weight.shape
    rows_total = 4 * parts[0].shape[0]
    f32 = jnp.float32
    return pl.pallas_call(
        functools.partial(encode_kernel, own),
        out_shape=(
            jax.ShapeDtypeStruct((rows_total, width // 2), jnp.bfloat16),
            jax.ShapeDtypeStruct((rows_total, width), jnp.bfloat16),
            jax.ShapeDtypeStruct((rows_total, count), f32),
            jax.ShapeDtypeStruct((rows_total, count), f32),
            jax.ShapeDtypeStruct((rows_total, 1), f32),
        ),
        in_specs=[whole()] * 6,
        out_specs=[whole()] * 5,
        scratch_shapes=[pltpu.VMEM((rows_total, width), f32), pltpu.VMEM((rows_total, count), f32)],
        compiler_params=pltpu.CompilerParams(vmem_limit_bytes=VMEM_BYTES),
        name="encode",
    )(*parts, weight, enc_bias.reshape(1, count))


def keep_kernel(rides, latents_ref, sharp_ref, weight_ref, *refs):
    half = weight_ref.shape[1] // 2
    latents = latents_ref[...]
    if rides:
        *refs, leaving_ref, staying_ref, packed_ref = refs
    *sources, mine_ref, gate_ref, norms_ref, pull_ref = refs
    here, _ = core_columns(half)
    mine_ref[...] = jnp.dot(
        latents.astype(jnp.bfloat16), weight_ref[:, here], preferred_element_type=jnp.float32
    )
    gate_ref[...] = jax.nn.sigmoid(sharp_ref[...])
    weight_f = weight_ref[...].astype(jnp.float32)
    squares = jnp.sum(weight_f * weight_f, axis=1, keepdims=True)
    squares = jnp.broadcast_to(squares, (squares.shape[0], 128)).T
    norms = jnp.sqrt(squares[:1] + 1e-06)
    norms_ref[...] = norms
    counts = jnp.sum(latents, axis=0, keepdims=True)
    pull = SPARSITY / (latents.shape[0] // 2) * counts / norms
    pull_ref[...] = jnp.broadcast_to(pull, squares.shape).T[:, :1]
    if rides:
        own = staying_ref.shape[1]
        shares = packed_ref.shape[1]
        below = len(sources) * own
        for index, ref in enumerate(sources):
            start = ref.shape[1] - 2 * shares
            value = ref[:, start:].astype(jnp.float32)
            staying_ref[index] = value[:own]
            rows = slice(index * own, (index + 1) * own)
            packed_ref[rows] = value[own:, :shares]
            rows = slice(below + index * own, below + (index + 1) * own)
            packed_ref[rows] = value[own:, shares:]
        leaving_ref[...] = packed_ref[...].astype(jnp.bfloat16)


def keep(latents, sharp, weight, sources, own, shares):
    rows_total, count = latents.shape
    width = weight.shape[1]
    f32 = jnp.float32
    out_shape = [
        jax.ShapeDtypeStruct((rows_total, width // 2), f32),
        jax.ShapeDtypeStruct((rows_total, count), f32),
        jax.ShapeDtypeStruct((1, count), f32),
        jax.ShapeDtypeStruct((count, 1), f32),
    ]
    scratch = []
    if sources:
        out_shape += [
            jax.ShapeDtypeStruct((rows_total, shares), jnp.bfloat16),
            jax.ShapeDtypeStruct((len(sources), own, 2 * shares), f32),
        ]
        scratch = [pltpu.VMEM((rows_total, shares), f32)]
    return pl.pallas_call(
        functools.partial(keep_kernel, bool(sources)),
        out_shape=out_shape,
        in_specs=[whole()] * (3 + len(sources)),
        out_specs=[whole()] * len(out_shape),
        scratch_shapes=scratch,
        compiler_params=pltpu.CompilerParams(vmem_limit_bytes=VMEM_BYTES),
        cost_estimate=pl.CostEstimate(
            flops=rows_total * count * width, bytes_accessed=count * width, transcendentals=0
        ),
        name="keep",
    )(latents, sharp, weight, *sources)


def merge_kernel(distances, total_ref, *refs):
    total = total_ref[...]
    for distance, ref in zip(distances, refs):
        total = total + flip_rows(ref[...].astype(jnp.float32), distance)
    *riders, sum_ref, sent_ref = refs[len(distances) :]
    sum_ref[...] = total
    half = total.shape[1]
    sent_ref[:, :half] = total.astype(jnp.bfloat16)
    for rider in riders:
        sent_ref[:, half:] = rider[...]


def merge(total, arrived, distances, riders=()):
    rows_total, half = total.shape
    wide = half + sum(rider.shape[1] for rider in riders)
    return pl.pallas_call(
        functools.partial(merge_kernel, distances),
        out_shape=(
            jax.ShapeDtypeStruct(total.shape, jnp.float32),
            jax.ShapeDtypeStruct((rows_total, wide), jnp.bfloat16),
        ),
        in_specs=[whole()] * (1 + len(arrived) + len(riders)),
        out_specs=[whole()] * 2,
        compiler_params=pltpu.CompilerParams(vmem_limit_bytes=VMEM_BYTES),
        name="merge",
    )(total, *arrived, *riders)


def settle_kernel(distance, total_ref, arrived_ref, rows_ref, scales_ref, bias_ref, grad_ref):
    rows_total, width = rows_ref.shape
    here, _ = core_columns(width // 2)
    arrived = arrived_ref[:, : width // 2].astype(jnp.float32)
    total = total_ref[...] + flip_rows(arrived, distance)
    target = rows_ref[:, here].astype(jnp.float32) * scales_ref[...]
    error = total + bias_ref[:, here] - target
    grad_ref[...] = (2.0 / (rows_total // 2) * error).astype(jnp.bfloat16)


def settle(total, arrived, rows, scales, dec_bias, distance):
    return pl.pallas_call(
        functools.partial(settle_kernel, distance),
        out_shape=jax.ShapeDtypeStruct(total.shape, jnp.bfloat16),
        in_specs=[whole()] * 5,
        out_specs=whole(),
        compiler_params=pltpu.CompilerParams(vmem_limit_bytes=VMEM_BYTES),
        name="settle",
    )(total, arrived, rows, scales, dec_bias.reshape(1, -1))


def early_kernel(grad_ref, weight_ref, norms_ref, out_ref):
    here, _ = core_columns(weight_ref.shape[1] // 2)
    batch_rows = grad_ref.shape[0] // 2
    out_ref[...] = (
        lax.dot_general(
            grad_ref[...], weight_ref[:, here], NT, preferred_element_type=jnp.float32
        )
        + SPARSITY / batch_rows * norms_ref[...]
    )


def early(grad_mine, weight, norms):
    rows_total, half = grad_mine.shape
    count = weight.shape[0]
    return pl.pallas_call(
        early_kernel,
        out_shape=jax.ShapeDtypeStruct((rows_total, count), jnp.float32),
        in_specs=[whole()] * 3,
        out_specs=whole(),
        compiler_params=pltpu.CompilerParams(vmem_limit_bytes=VMEM_BYTES),
        cost_estimate=pl.CostEstimate(
            flops=2 * rows_total * count * half, bytes_accessed=count * half, transcendentals=0
        ),
        name="early",
    )(grad_mine, weight, norms)


def finish_kernel(
    tile,
    span,
    rides,
    turn,
    mine_ref,
    other_ref,
    early_ref,
    rows_ref,
    weight_ref,
    latents_ref,
    gate_ref,
    scales_ref,
    pull_ref,
    *refs,
):
    if rides:
        arrived_ref, staying_ref, weight_grad_hbm, bias_grad_hbm, dec_grad_hbm, next_hbm = refs[:6]
        *refs, blocks_ref, line_ref, next_ref = refs[6:]
    else:
        weight_grad_hbm, bias_grad_hbm, dec_grad_hbm, *refs = refs
    grad_ref, staged_ref, bias_ref, dec_ref, sums_ref, left_ref, sems = refs
    rows_total, width = rows_ref.shape
    shares = dec_grad_hbm.shape[0]
    count = width // tile
    core = lax.axis_index("latent")
    here, there = core_columns(width // 2)
    grad_latents = early_ref[...] + lax.dot_general(
        other_ref[...], weight_ref[:, there], NT, preferred_element_type=jnp.float32
    )
    grad_ref[:, here] = mine_ref[...]
    grad_ref[:, there] = other_ref[...]
    grad_pre = grad_latents * gate_ref[...]
    bias_ref[...] = jnp.sum(grad_pre, axis=0, keepdims=True)
    bias_copy = pltpu.make_async_copy(bias_ref, bias_grad_hbm, sems.at[count])
    bias_copy.start()
    left = jnp.concatenate([grad_pre * scales_ref[...], latents_ref[...]], axis=0)
    left_ref[...] = left.T.astype(jnp.bfloat16)

    sums = jnp.sum(grad_ref[...].astype(jnp.float32), axis=0, keepdims=True)
    sums_ref[:, :width] = jnp.broadcast_to(sums, (8, width))
    sums_ref[:, width:] = jnp.zeros((8, span), jnp.float32)
    offset = lax.axis_index(("dp", "latent")) * shares
    lead = lax.rem(offset, 128)
    window = sums_ref[:, pl.ds(pl.multiple_of(offset - lead, 128), span)]
    window = pltpu.roll(window, lax.rem(span - lead, span), 1)
    dec_ref[...] = window[0, :shares]
    dec_copy = pltpu.make_async_copy(dec_ref, dec_grad_hbm, sems.at[count + 1])
    dec_copy.start()

    if rides:
        near, own, columns = staying_ref.shape
        came = arrived_ref[:, width // 2 :].astype(jnp.float32)
        for index in range(near):
            blocks_ref[index] = staying_ref[index]
            rows = slice(index * own, (index + 1) * own)
            blocks_ref[near + index, :, :shares] = came[rows]
            rows = slice((near + index) * own, (near + index + 1) * own)
            blocks_ref[near + index, :, shares:] = came[rows]
        place = lax.axis_index("dp")
        for source in range(2 * near):
            away = place ^ source
            away = away ^ (turn * (away // near))
            line_ref[:, source * columns : (source + 1) * columns] = blocks_ref[away]
        next_ref[...] = line_ref[...].astype(jnp.bfloat16)
        next_copy = pltpu.make_async_copy(next_ref, next_hbm, sems.at[count + 2])
        next_copy.start()

    copies = [
        pltpu.make_async_copy(
            staged_ref.at[:, pl.ds(index * tile, tile)],
            weight_grad_hbm.at[:, pl.ds(index * tile, tile)],
            sems.at[index],
        )
        for index in range(count)
    ]

    @pl.loop(0, 1 + core // 2)
    def _(_):
        pull = pull_ref[...]
        for index in range(count):
            columns = slice(index * tile, (index + 1) * tile)
            right = jnp.concatenate([rows_ref[:, columns], grad_ref[:, columns]], axis=0)
            total = jnp.dot(left_ref[...], right, preferred_element_type=jnp.float32)
            total = total + pull * weight_ref[:, columns].astype(jnp.float32)
            staged_ref[:, columns] = total.astype(jnp.bfloat16)
            copies[index].start()

    for copy in copies:
        copy.wait()
    bias_copy.wait()
    dec_copy.wait()
    if rides:
        next_copy.wait()


def finish(mine, other, early_sum, rows, weight, latents, gate, scales, pull, shares, riders, turn):
    rows_total, width = rows.shape
    count = weight.shape[0]
    tile = 768
    span = (shares + 127 + 127) // 128 * 128
    f32 = jnp.float32
    out_shape = [
        jax.ShapeDtypeStruct((count, width), jnp.bfloat16),
        jax.ShapeDtypeStruct((1, count), f32),
        jax.ShapeDtypeStruct((shares,), f32),
    ]
    scratch = [
        pltpu.VMEM((rows_total, width), jnp.bfloat16),
        pltpu.VMEM((count, width), jnp.bfloat16),
        pltpu.VMEM((1, count), f32),
        pltpu.VMEM((shares,), f32),
        pltpu.VMEM((8, width + span), f32),
        pltpu.VMEM((count, 2 * rows_total), jnp.bfloat16),
        pltpu.SemaphoreType.DMA((width // tile + 3,)),
    ]
    if riders:
        near, own, columns = riders[1].shape
        out_shape.append(jax.ShapeDtypeStruct((own, width), jnp.bfloat16))
        scratch += [
            pltpu.VMEM((2 * near, own, columns), f32),
            pltpu.VMEM((own, width), f32),
            pltpu.VMEM((own, width), jnp.bfloat16),
        ]
    return pl.pallas_call(
        functools.partial(finish_kernel, tile, span, bool(riders), turn),
        out_shape=out_shape,
        in_specs=[whole()] * (9 + len(riders)),
        out_specs=[whole(pl.ANY)] * len(out_shape),
        scratch_shapes=scratch,
        compiler_params=pltpu.CompilerParams(vmem_limit_bytes=VMEM_BYTES),
        name="finish",
    )(mine, other, early_sum, rows, weight, latents, gate, scales, pull, *riders)


def shuffle_rest(riders, dp, own, columns):
    place = lax.axis_index("dp")
    distance = 4
    while distance < dp:
        split = riders.reshape((-1, 2) + riders.shape[1:])
        riders = jnp.concatenate([split[:, 0], exchange(split[:, 1], "dp", distance)], axis=1)
        distance *= 2
    riders = riders[0]
    bit = 1
    while bit < dp:
        pairs = riders.reshape(dp // (2 * bit), 2, bit * own * columns)
        pairs = jnp.where(place & bit == 0, pairs, pairs[:, ::-1])
        riders = pairs.reshape(dp, own, columns)
        bit *= 2
    return riders.transpose(1, 0, 2).reshape(own, dp * columns)


def per_device(cur_rows, cached_rows, shuffle_perm, weight, enc_bias, dec_bias):
    dp = lax.axis_size("dp")
    rest = dp // 4
    own, width = cur_rows.shape
    columns = cached_rows.shape[1]
    count = weight.shape[0]
    shares = width // (2 * dp)

    rides = rest == 2
    turn = 2 if rides else 0

    came = exchange(cur_rows, "dp", 4)
    ordered, cur_copy, weight = order(cur_rows, cached_rows, shuffle_perm, weight, turn)
    near = jnp.concatenate([cur_copy, came], axis=0)
    distance = 8
    while distance < dp:
        near = jnp.concatenate([near, exchange(near, "dp", distance)], axis=0)
        distance *= 2
    ordered = ordered.reshape(4, rest * own, columns)
    messages = [None] + [
        jnp.concatenate([near, ordered[low]], axis=1) for low in range(1, 4)
    ]
    roles = (1, 3)
    core = lax.axis_index("latent")
    pairs = [(2 * k + c, 2 * (k ^ roles[c]) + c) for k in range(dp) for c in range(2)]
    parts = [near, None, None, None]
    parts[2] = exchange(messages[2], "dp", 2)
    fetched = lax.ppermute(
        jnp.where(core == 0, messages[roles[0]], messages[roles[1]]), ("dp", "latent"), pairs
    )
    handed = exchange(fetched, "latent", 1)
    parts[roles[0]] = jnp.where(core == 0, fetched, handed)
    parts[roles[1]] = jnp.where(core == 0, handed, fetched)

    send, gathered, latents, sharp, scales = encode(parts, weight, enc_bias, own)
    came = exchange(send, "latent", 1)
    sources = [ordered[0]] + parts[1:] if rides else []
    mine, gate, norms, pull, *riders = keep(latents, sharp, weight, sources, own, shares)

    total = mine + came.astype(jnp.float32)
    sent = total.astype(jnp.bfloat16)
    lows = (1, 2, 3)
    total, sent = merge(
        total,
        [exchange(sent, "dp", low) for low in lows],
        tuple(low * rest * own for low in lows),
        riders[:1],
    )
    distance = 4
    while distance < dp:
        arrived = exchange(sent, "dp", distance + turn)
        row_distance = distance // 4 * own + turn * rest * own
        if 2 * distance < dp:
            total, sent = merge(total, [arrived], (row_distance,))
        else:
            grad_mine = settle(total, arrived, gathered, scales, dec_bias, row_distance)
        distance *= 2

    grad_other = exchange(grad_mine, "latent", 1)
    early_sum = early(grad_mine, weight, norms)
    weight_grad, enc_bias_grad, dec_bias_grad, *shuffled = finish(
        grad_mine,
        grad_other,
        early_sum,
        gathered,
        weight,
        latents,
        gate,
        scales,
        pull,
        shares,
        (arrived, riders[1]) if rides else (),
        turn,
    )
    if rides:
        next_batch = shuffled[0]
    else:
        riders = jnp.stack([ordered[0]] + [part[:, width:] for part in parts[1:]])
        riders = riders.reshape(4, rest, own, columns).transpose(1, 0, 2, 3)
        next_batch = shuffle_rest(riders, dp, own, columns)
    return (weight_grad, enc_bias_grad.reshape(count), dec_bias_grad, next_batch)


def solution(mesh):
    return jax.shard_map(
        per_device,
        mesh=mesh,
        in_specs=(
            P(("group", "dp"), None),
            P("group", "dp"),
            P("group"),
            P(("group", "dp", "latent"), None),
            P(("group", "dp", "latent")),
            P("group"),
        ),
        out_specs=(
            P(("group", "dp", "latent"), None),
            P(("group", "dp", "latent")),
            P(("group", "dp", "latent")),
            P(("group", "dp"), None),
        ),
        check_vma=False,
    )
```

```python
import functools

import jax
import jax.numpy as jnp
from jax import lax
from jax.experimental import pallas as pl
from jax.experimental.pallas import tpu as pltpu
from jax.sharding import PartitionSpec as P

SPARSITY = 4.0
SHARP = 4.0
VMEM_BYTES = 16 * 1024 * 1024
NT = (((1,), (1,)), ((), ()))
TN = (((0,), (0,)), ((), ()))


def whole(space=pltpu.VMEM):
    return pl.BlockSpec(memory_space=space)


def exchange(value, axis, distance):
    size = lax.axis_size(axis)
    return lax.ppermute(value, axis, [(k, k ^ distance) for k in range(size)])


def core_columns(half):
    core = lax.axis_index("latent") ^ (lax.axis_index("dp") // 4 % 2)
    here = pl.ds(pl.multiple_of(core * half, 128), half)
    there = pl.ds(pl.multiple_of((1 - core) * half, 128), half)
    return here, there


def across(value, distance):
    size = lax.axis_size("dp")
    pairs = [(2 * k + c, 2 * (k ^ distance) + 1 - c) for k in range(size) for c in range(2)]
    return lax.ppermute(value, ("dp", "latent"), pairs)


def flip_rows(value, distance):
    count = value.shape[0]
    row = lax.broadcasted_iota(jnp.int32, value.shape, 0)
    bit = 1
    while bit <= distance:
        if distance & bit:
            up = pltpu.roll(value, count - bit, 0)
            down = pltpu.roll(value, bit, 0)
            value = jnp.where(row & bit == 0, up, down)
        bit *= 2
    return value


def order_kernel(
    turn,
    cur_hbm,
    cached_hbm,
    perm_hbm,
    weight_hbm,
    out_ref,
    cur_ref,
    weight_ref,
    cached_ref,
    perm_ref,
    sems,
):
    row_total, columns = cached_ref.shape
    own = cur_ref.shape[0]
    dp = row_total // own
    fetches = [
        pltpu.make_async_copy(cached_hbm, cached_ref, sems.at[0]),
        pltpu.make_async_copy(perm_hbm, perm_ref, sems.at[1]),
        pltpu.make_async_copy(cur_hbm, cur_ref, sems.at[2]),
        pltpu.make_async_copy(weight_hbm, weight_ref, sems.at[3]),
    ]
    for fetch in fetches:
        fetch.start()
    row = lax.broadcasted_iota(jnp.int32, (row_total, row_total), 0)
    rest = dp // 4
    low, high = row // (rest * own), row // own % rest
    distance = (low ^ (turn * high)) + 4 * high
    wanted = (distance ^ lax.axis_index("dp")) * own + row % own
    for fetch in fetches[:2]:
        fetch.wait()
    selector = (jnp.broadcast_to(perm_ref[...], row.shape) == wanted).astype(jnp.bfloat16)
    out_ref[...] = jnp.dot(
        selector, cached_ref[...], preferred_element_type=jnp.float32
    ).astype(jnp.bfloat16)
    for fetch in fetches[2:]:
        fetch.wait()


def order(cur_rows, cached_rows, shuffle_perm, weight, turn):
    row_total, columns = cached_rows.shape
    return pl.pallas_call(
        functools.partial(order_kernel, turn),
        out_shape=(
            jax.ShapeDtypeStruct((row_total, columns), jnp.bfloat16),
            jax.ShapeDtypeStruct(cur_rows.shape, jnp.bfloat16),
            jax.ShapeDtypeStruct(weight.shape, jnp.bfloat16),
        ),
        in_specs=[whole(pl.ANY)] * 4,
        out_specs=[whole()] * 3,
        scratch_shapes=[
            pltpu.VMEM((row_total, columns), jnp.bfloat16),
            pltpu.VMEM((1, row_total), jnp.int32),
            pltpu.SemaphoreType.DMA((4,)),
        ],
        compiler_params=pltpu.CompilerParams(vmem_limit_bytes=VMEM_BYTES),
        cost_estimate=pl.CostEstimate(flops=4000000, bytes_accessed=2000000, transcendentals=0),
        name="order",
    )(
        *(
            pltpu.with_memory_space_constraint(value, pltpu.MemorySpace.HBM)
            for value in (cur_rows, cached_rows, shuffle_perm.reshape(1, row_total), weight)
        )
    )


def encode_kernel(
    own,
    first_ref,
    second_ref,
    third_ref,
    fourth_ref,
    weight_ref,
    bias_ref,
    send_ref,
    rows_ref,
    latents_ref,
    sharp_ref,
    scales_ref,
    rows_f_ref,
    scaled_ref,
):
    rows_total, width = rows_f_ref.shape
    batch_rows = rows_total // 2
    part = rows_total // 4
    for index, ref in enumerate((first_ref, second_ref, third_ref, fourth_ref)):
        value = ref[...].astype(jnp.float32)
        rows_f_ref[index * part : (index + 1) * part] = value[:, :width]
    rows_f = rows_f_ref[...]
    rows = rows_f.astype(jnp.bfloat16)
    rows_ref[...] = rows
    projected = lax.dot_general(rows, weight_ref[...], NT, preferred_element_type=jnp.float32)
    squares = jnp.sum(rows_f * rows_f, axis=1, keepdims=True)
    row = lax.broadcasted_iota(jnp.int32, (rows_total, 1), 0)
    rest = part // own
    near = row // own % rest < rest // 2
    here = jnp.sum(jnp.where(near, squares, 0.0), axis=0, keepdims=True) / batch_rows
    far = jnp.sum(jnp.where(near, 0.0, squares), axis=0, keepdims=True) / batch_rows
    scales = jnp.sqrt(width / jnp.where(near, here, far))
    scales_ref[...] = scales
    scaled_ref[...] = scales * projected

    @pl.loop(0, 1 + lax.axis_index("latent") // 2)
    def _(_):
        sharp = SHARP * (scaled_ref[...] + bias_ref[...])
        latents = jax.nn.softplus(sharp) / SHARP
        sharp_ref[...] = sharp
        latents_ref[...] = latents
        _, there = core_columns(width // 2)
        send_ref[...] = jnp.dot(
            latents.astype(jnp.bfloat16),
            weight_ref[:, there],
            preferred_element_type=jnp.float32,
        ).astype(jnp.bfloat16)


def encode(parts, weight, enc_bias, own):
    count, width = weight.shape
    rows_total = 4 * parts[0].shape[0]
    f32 = jnp.float32
    return pl.pallas_call(
        functools.partial(encode_kernel, own),
        out_shape=(
            jax.ShapeDtypeStruct((rows_total, width // 2), jnp.bfloat16),
            jax.ShapeDtypeStruct((rows_total, width), jnp.bfloat16),
            jax.ShapeDtypeStruct((rows_total, count), f32),
            jax.ShapeDtypeStruct((rows_total, count), f32),
            jax.ShapeDtypeStruct((rows_total, 1), f32),
        ),
        in_specs=[whole()] * 6,
        out_specs=[whole()] * 5,
        scratch_shapes=[pltpu.VMEM((rows_total, width), f32), pltpu.VMEM((rows_total, count), f32)],
        compiler_params=pltpu.CompilerParams(vmem_limit_bytes=VMEM_BYTES),
        name="encode",
    )(*parts, weight, enc_bias.reshape(1, count))


def keep_kernel(rides, latents_ref, sharp_ref, weight_ref, *refs):
    half = weight_ref.shape[1] // 2
    latents = latents_ref[...]
    if rides:
        *refs, leaving_ref, staying_ref, packed_ref = refs
    *sources, mine_ref, gate_ref, norms_ref, pull_ref = refs
    here, _ = core_columns(half)
    mine_ref[...] = jnp.dot(
        latents.astype(jnp.bfloat16), weight_ref[:, here], preferred_element_type=jnp.float32
    )
    gate_ref[...] = jax.nn.sigmoid(sharp_ref[...])
    weight_f = weight_ref[...].astype(jnp.float32)
    squares = jnp.sum(weight_f * weight_f, axis=1, keepdims=True)
    squares = jnp.broadcast_to(squares, (squares.shape[0], 128)).T
    norms = jnp.sqrt(squares[:1] + 1e-06)
    norms_ref[...] = norms
    counts = jnp.sum(latents, axis=0, keepdims=True)
    pull = SPARSITY / (latents.shape[0] // 2) * counts / norms
    pull_ref[...] = jnp.broadcast_to(pull, squares.shape).T[:, :1]
    if rides:
        own = staying_ref.shape[1]
        shares = packed_ref.shape[1]
        below = len(sources) * own
        for index, ref in enumerate(sources):
            start = ref.shape[1] - 2 * shares
            value = ref[:, start:].astype(jnp.float32)
            staying_ref[index] = value[:own]
            rows = slice(index * own, (index + 1) * own)
            packed_ref[rows] = value[own:, :shares]
            rows = slice(below + index * own, below + (index + 1) * own)
            packed_ref[rows] = value[own:, shares:]
        leaving_ref[...] = packed_ref[...].astype(jnp.bfloat16)


def keep(latents, sharp, weight, sources, own, shares):
    rows_total, count = latents.shape
    width = weight.shape[1]
    f32 = jnp.float32
    out_shape = [
        jax.ShapeDtypeStruct((rows_total, width // 2), f32),
        jax.ShapeDtypeStruct((rows_total, count), f32),
        jax.ShapeDtypeStruct((1, count), f32),
        jax.ShapeDtypeStruct((count, 1), f32),
    ]
    scratch = []
    if sources:
        out_shape += [
            jax.ShapeDtypeStruct((rows_total, shares), jnp.bfloat16),
            jax.ShapeDtypeStruct((len(sources), own, 2 * shares), f32),
        ]
        scratch = [pltpu.VMEM((rows_total, shares), f32)]
    return pl.pallas_call(
        functools.partial(keep_kernel, bool(sources)),
        out_shape=out_shape,
        in_specs=[whole()] * (3 + len(sources)),
        out_specs=[whole()] * len(out_shape),
        scratch_shapes=scratch,
        compiler_params=pltpu.CompilerParams(vmem_limit_bytes=VMEM_BYTES),
        cost_estimate=pl.CostEstimate(
            flops=rows_total * count * width, bytes_accessed=count * width, transcendentals=0
        ),
        name="keep",
    )(latents, sharp, weight, *sources)


def merge_kernel(distances, total_ref, *refs):
    total = total_ref[...]
    for distance, ref in zip(distances, refs):
        total = total + flip_rows(ref[...].astype(jnp.float32), distance)
    *riders, sum_ref, sent_ref = refs[len(distances) :]
    sum_ref[...] = total
    half = total.shape[1]
    sent_ref[:, :half] = total.astype(jnp.bfloat16)
    for rider in riders:
        sent_ref[:, half:] = rider[...]


def merge(total, arrived, distances, riders=()):
    rows_total, half = total.shape
    wide = half + sum(rider.shape[1] for rider in riders)
    return pl.pallas_call(
        functools.partial(merge_kernel, distances),
        out_shape=(
            jax.ShapeDtypeStruct(total.shape, jnp.float32),
            jax.ShapeDtypeStruct((rows_total, wide), jnp.bfloat16),
        ),
        in_specs=[whole()] * (1 + len(arrived) + len(riders)),
        out_specs=[whole()] * 2,
        compiler_params=pltpu.CompilerParams(vmem_limit_bytes=VMEM_BYTES),
        name="merge",
    )(total, *arrived, *riders)


def settle_kernel(distance, total_ref, arrived_ref, rows_ref, scales_ref, bias_ref, grad_ref):
    rows_total, width = rows_ref.shape
    here, _ = core_columns(width // 2)
    arrived = arrived_ref[:, : width // 2].astype(jnp.float32)
    total = total_ref[...] + flip_rows(arrived, distance)
    target = rows_ref[:, here].astype(jnp.float32) * scales_ref[...]
    error = total + bias_ref[:, here] - target
    grad_ref[...] = (2.0 / (rows_total // 2) * error).astype(jnp.bfloat16)


def settle(total, arrived, rows, scales, dec_bias, distance):
    return pl.pallas_call(
        functools.partial(settle_kernel, distance),
        out_shape=jax.ShapeDtypeStruct(total.shape, jnp.bfloat16),
        in_specs=[whole()] * 5,
        out_specs=whole(),
        compiler_params=pltpu.CompilerParams(vmem_limit_bytes=VMEM_BYTES),
        name="settle",
    )(total, arrived, rows, scales, dec_bias.reshape(1, -1))


def early_kernel(grad_ref, weight_ref, norms_ref, out_ref):
    here, _ = core_columns(weight_ref.shape[1] // 2)
    batch_rows = grad_ref.shape[0] // 2
    out_ref[...] = (
        lax.dot_general(
            grad_ref[...], weight_ref[:, here], NT, preferred_element_type=jnp.float32
        )
        + SPARSITY / batch_rows * norms_ref[...]
    )


def early(grad_mine, weight, norms):
    rows_total, half = grad_mine.shape
    count = weight.shape[0]
    return pl.pallas_call(
        early_kernel,
        out_shape=jax.ShapeDtypeStruct((rows_total, count), jnp.float32),
        in_specs=[whole()] * 3,
        out_specs=whole(),
        compiler_params=pltpu.CompilerParams(vmem_limit_bytes=VMEM_BYTES),
        cost_estimate=pl.CostEstimate(
            flops=2 * rows_total * count * half, bytes_accessed=count * half, transcendentals=0
        ),
        name="early",
    )(grad_mine, weight, norms)


def finish_kernel(
    tile,
    span,
    rides,
    turn,
    mine_ref,
    other_ref,
    early_ref,
    rows_ref,
    weight_ref,
    latents_ref,
    gate_ref,
    scales_ref,
    pull_ref,
    *refs,
):
    if rides:
        arrived_ref, staying_ref, weight_grad_hbm, bias_grad_hbm, dec_grad_hbm, next_hbm = refs[:6]
        *refs, blocks_ref, line_ref, next_ref = refs[6:]
    else:
        weight_grad_hbm, bias_grad_hbm, dec_grad_hbm, *refs = refs
    grad_ref, staged_ref, bias_ref, dec_ref, sums_ref, left_ref, sems = refs
    rows_total, width = rows_ref.shape
    shares = dec_grad_hbm.shape[0]
    count = width // tile
    core = lax.axis_index("latent")
    here, there = core_columns(width // 2)
    grad_latents = early_ref[...] + lax.dot_general(
        other_ref[...], weight_ref[:, there], NT, preferred_element_type=jnp.float32
    )
    grad_ref[:, here] = mine_ref[...]
    grad_ref[:, there] = other_ref[...]
    grad_pre = grad_latents * gate_ref[...]
    bias_ref[...] = jnp.sum(grad_pre, axis=0, keepdims=True)
    bias_copy = pltpu.make_async_copy(bias_ref, bias_grad_hbm, sems.at[count])
    bias_copy.start()
    left = jnp.concatenate([grad_pre * scales_ref[...], latents_ref[...]], axis=0)
    left_ref[...] = left.T.astype(jnp.bfloat16)

    sums = jnp.sum(grad_ref[...].astype(jnp.float32), axis=0, keepdims=True)
    sums_ref[:, :width] = jnp.broadcast_to(sums, (8, width))
    sums_ref[:, width:] = jnp.zeros((8, span), jnp.float32)
    offset = lax.axis_index(("dp", "latent")) * shares
    lead = lax.rem(offset, 128)
    window = sums_ref[:, pl.ds(pl.multiple_of(offset - lead, 128), span)]
    window = pltpu.roll(window, lax.rem(span - lead, span), 1)
    dec_ref[...] = window[0, :shares]
    dec_copy = pltpu.make_async_copy(dec_ref, dec_grad_hbm, sems.at[count + 1])
    dec_copy.start()

    if rides:
        near, own, columns = staying_ref.shape
        came = arrived_ref[:, width // 2 :].astype(jnp.float32)
        for index in range(near):
            blocks_ref[index] = staying_ref[index]
            rows = slice(index * own, (index + 1) * own)
            blocks_ref[near + index, :, :shares] = came[rows]
            rows = slice((near + index) * own, (near + index + 1) * own)
            blocks_ref[near + index, :, shares:] = came[rows]
        place = lax.axis_index("dp")
        for source in range(2 * near):
            away = place ^ source
            away = away ^ (turn * (away // near))
            line_ref[:, source * columns : (source + 1) * columns] = blocks_ref[away]
        next_ref[...] = line_ref[...].astype(jnp.bfloat16)
        next_copy = pltpu.make_async_copy(next_ref, next_hbm, sems.at[count + 2])
        next_copy.start()

    copies = [
        pltpu.make_async_copy(
            staged_ref.at[:, pl.ds(index * tile, tile)],
            weight_grad_hbm.at[:, pl.ds(index * tile, tile)],
            sems.at[index],
        )
        for index in range(count)
    ]

    @pl.loop(0, 1 + core // 2)
    def _(_):
        pull = pull_ref[...]
        for index in range(count):
            columns = slice(index * tile, (index + 1) * tile)
            right = jnp.concatenate([rows_ref[:, columns], grad_ref[:, columns]], axis=0)
            total = jnp.dot(left_ref[...], right, preferred_element_type=jnp.float32)
            total = total + pull * weight_ref[:, columns].astype(jnp.float32)
            staged_ref[:, columns] = total.astype(jnp.bfloat16)
            copies[index].start()

    for copy in copies:
        copy.wait()
    bias_copy.wait()
    dec_copy.wait()
    if rides:
        next_copy.wait()


def finish(mine, other, early_sum, rows, weight, latents, gate, scales, pull, shares, riders, turn):
    rows_total, width = rows.shape
    count = weight.shape[0]
    tile = 768
    span = (shares + 127 + 127) // 128 * 128
    f32 = jnp.float32
    out_shape = [
        jax.ShapeDtypeStruct((count, width), jnp.bfloat16),
        jax.ShapeDtypeStruct((1, count), f32),
        jax.ShapeDtypeStruct((shares,), f32),
    ]
    scratch = [
        pltpu.VMEM((rows_total, width), jnp.bfloat16),
        pltpu.VMEM((count, width), jnp.bfloat16),
        pltpu.VMEM((1, count), f32),
        pltpu.VMEM((shares,), f32),
        pltpu.VMEM((8, width + span), f32),
        pltpu.VMEM((count, 2 * rows_total), jnp.bfloat16),
        pltpu.SemaphoreType.DMA((width // tile + 3,)),
    ]
    if riders:
        near, own, columns = riders[1].shape
        out_shape.append(jax.ShapeDtypeStruct((own, width), jnp.bfloat16))
        scratch += [
            pltpu.VMEM((2 * near, own, columns), f32),
            pltpu.VMEM((own, width), f32),
            pltpu.VMEM((own, width), jnp.bfloat16),
        ]
    return pl.pallas_call(
        functools.partial(finish_kernel, tile, span, bool(riders), turn),
        out_shape=out_shape,
        in_specs=[whole()] * (9 + len(riders)),
        out_specs=[whole(pl.ANY)] * len(out_shape),
        scratch_shapes=scratch,
        compiler_params=pltpu.CompilerParams(vmem_limit_bytes=VMEM_BYTES),
        name="finish",
    )(mine, other, early_sum, rows, weight, latents, gate, scales, pull, *riders)


def shuffle_rest(riders, dp, own, columns):
    place = lax.axis_index("dp")
    distance = 4
    while distance < dp:
        split = riders.reshape((-1, 2) + riders.shape[1:])
        riders = jnp.concatenate([split[:, 0], exchange(split[:, 1], "dp", distance)], axis=1)
        distance *= 2
    riders = riders[0]
    bit = 1
    while bit < dp:
        pairs = riders.reshape(dp // (2 * bit), 2, bit * own * columns)
        pairs = jnp.where(place & bit == 0, pairs, pairs[:, ::-1])
        riders = pairs.reshape(dp, own, columns)
        bit *= 2
    return riders.transpose(1, 0, 2).reshape(own, dp * columns)


def per_device(cur_rows, cached_rows, shuffle_perm, weight, enc_bias, dec_bias):
    dp = lax.axis_size("dp")
    rest = dp // 4
    own, width = cur_rows.shape
    columns = cached_rows.shape[1]
    count = weight.shape[0]
    shares = width // (2 * dp)

    rides = rest == 2
    turn = 2 if rides else 0

    came = across(cur_rows, 4)
    ordered, cur_copy, weight = order(cur_rows, cached_rows, shuffle_perm, weight, turn)
    near = jnp.concatenate([cur_copy, came], axis=0)
    distance = 8
    while distance < dp:
        near = jnp.concatenate([near, exchange(near, "dp", distance)], axis=0)
        distance *= 2
    ordered = ordered.reshape(4, rest * own, columns)
    messages = [None] + [
        jnp.concatenate([near, ordered[low]], axis=1) for low in range(1, 4)
    ]
    roles = (1, 3)
    core = lax.axis_index("latent")
    pairs = [(2 * k + c, 2 * (k ^ roles[1 - c]) + 1 - c) for k in range(dp) for c in range(2)]
    parts = [near, None, None, None]
    parts[2] = across(messages[2], 2)
    fetched = lax.ppermute(
        jnp.where(core == 0, messages[roles[1]], messages[roles[0]]), ("dp", "latent"), pairs
    )
    handed = exchange(fetched, "latent", 1)
    parts[roles[0]] = jnp.where(core == 0, fetched, handed)
    parts[roles[1]] = jnp.where(core == 0, handed, fetched)

    send, gathered, latents, sharp, scales = encode(parts, weight, enc_bias, own)
    came = exchange(send, "latent", 1)
    sources = [ordered[0]] + parts[1:] if rides else []
    mine, gate, norms, pull, *riders = keep(latents, sharp, weight, sources, own, shares)

    total = mine + came.astype(jnp.float32)
    sent = total.astype(jnp.bfloat16)
    lows = (1, 2, 3)
    total, sent = merge(
        total,
        [exchange(sent, "dp", low) for low in lows],
        tuple(low * rest * own for low in lows),
        riders[:1],
    )
    distance = 4
    while distance < dp:
        arrived = (
            across(sent, distance + turn)
            if distance == 4
            else exchange(sent, "dp", distance + turn)
        )
        row_distance = distance // 4 * own + turn * rest * own
        if 2 * distance < dp:
            total, sent = merge(total, [arrived], (row_distance,))
        else:
            grad_mine = settle(total, arrived, gathered, scales, dec_bias, row_distance)
        distance *= 2

    grad_other = exchange(grad_mine, "latent", 1)
    early_sum = early(grad_mine, weight, norms)
    weight_grad, enc_bias_grad, dec_bias_grad, *shuffled = finish(
        grad_mine,
        grad_other,
        early_sum,
        gathered,
        weight,
        latents,
        gate,
        scales,
        pull,
        shares,
        (arrived, riders[1]) if rides else (),
        turn,
    )
    if rides:
        next_batch = shuffled[0]
    else:
        riders = jnp.stack([ordered[0]] + [part[:, width:] for part in parts[1:]])
        riders = riders.reshape(4, rest, own, columns).transpose(1, 0, 2, 3)
        next_batch = shuffle_rest(riders, dp, own, columns)
    return (weight_grad, enc_bias_grad.reshape(count), dec_bias_grad, next_batch)


def solution(mesh):
    return jax.shard_map(
        per_device,
        mesh=mesh,
        in_specs=(
            P(("group", "dp"), None),
            P("group", "dp"),
            P("group"),
            P(("group", "dp", "latent"), None),
            P(("group", "dp", "latent")),
            P("group"),
        ),
        out_specs=(
            P(("group", "dp", "latent"), None),
            P(("group", "dp", "latent")),
            P(("group", "dp", "latent")),
            P(("group", "dp"), None),
        ),
        check_vma=False,
    )
```
